512 devices in a mesh: space: 64 (over z, y), tensor: 8 (over x, core).
Axes of the slice: x: 4, y: 8, z: 8, core: 2. Of those that a mesh axis runs over, the one named last changes fastest.
Arguments:
- tokens: bfloat16 [57344, 1024], P('space', 'tensor'), may hold values from -16 to 16
- first_weight: bfloat16 [1024, 1024], P(None, 'tensor'), may hold values from -0.1875 to 0.1875
- second_weight: bfloat16 [1024, 1024], P(None, 'tensor'), may hold values from -0.1875 to 0.1875
- head_weight: bfloat16 [352, 1024], P('tensor'), may hold values from -0.1875 to 0.1875
- targets: float32 [352, 57344], P('tensor', 'space'), may hold values from -6 to 6
- land_mask: int32 [4, 57344], P(None, 'space'), may hold values from 0 to 1, as said below
- variable_kind: int32 [88], P('tensor'), may hold values from 0 to 2
- loss_scale: float32 [], replicated, may hold values from 2523136 to 20185088
Outputs:
- loss: float32 [], replicated
- token_grad: float32 [57344, 1024], P('space', 'tensor')
- first_grad: float32 [1024, 1024], P('space', 'tensor')
- second_grad: float32 [1024, 1024], P('space', 'tensor')
- head_grad: float32 [352, 1024], P('tensor', 'space')
The draws below stay inside these ranges and needn't reach their ends.
Inputs may be any that keep to these rules, and one draw needn't show every extreme that they name: `land_mask`: every aligned group of 8 entries along the last dimension holds at least one 1 and one 0. `variable_kind`: 0 scores a variable on all cells, 1 on land cells, 2 on ocean cells.
All inputs are finite; a program needn't handle non-finite values.
Results may differ from the reference program's by a relative error of at most 0.0056.
Values may be sent and summed in bfloat16 or wider, within the bound.
No kernel may reach another device: no remote copies, remote signals or barrier semaphores. Data moves between devices by JAX's collectives and lax.ppermute only.
A program may use at most 64 MiB of HBM per device.

```python
import math
import jax
import jax.numpy as jnp
from jax import lax

D = 1024
V = 88
PP = 4
LONP = 224
TOKENS = 57344
COLS = 352


def draw_land_mask(key, part):
    level_key = jax.random.fold_in(key, 21)
    band_key = jax.random.fold_in(key, 22)
    sector_key = jax.random.fold_in(key, 23)
    cell_key = jax.random.fold_in(key, 24)
    first = jax.random.fold_in(key, 25)
    second = jax.random.fold_in(key, 26)
    low_level = jax.random.randint(jax.random.fold_in(level_key, 1), (), 4, 21)
    high_level = jax.random.randint(jax.random.fold_in(level_key, 2), (), 55, 76)
    picker = jax.random.randint(jax.random.fold_in(level_key, 3), (), 0, 2)
    level = jnp.where(picker == 0, low_level, high_level).astype(jnp.int32)
    band_count = TOKENS // LONP
    band_shift = jax.random.randint(band_key, (band_count,), -25, 26).astype(jnp.int32)
    sector_shift = jax.random.randint(sector_key, (8,), -15, 16).astype(jnp.int32)
    position = jnp.arange(TOKENS, dtype=jnp.int32)
    band_index = position // LONP
    sector_index = position % LONP // (LONP // 8)
    chance = jnp.clip(level + band_shift[band_index] + sector_shift[sector_index], 2, 95).astype(jnp.int32)
    rolled = jax.random.randint(cell_key, (PP, TOKENS), 0, 100).astype(jnp.int32)
    base = (rolled < chance[None, :]).astype(jnp.int32)
    blocks = TOKENS // 8
    base = base.reshape(PP, blocks, 8)
    where_one = jax.random.randint(first, (PP, blocks, 1), 0, 8).astype(jnp.int32)
    where_zero = (where_one + jax.random.randint(second, (PP, blocks, 1), 1, 8).astype(jnp.int32)) % 8
    places = jnp.arange(8, dtype=jnp.int32)[None, None, :]
    base = jnp.where(places == where_one, 1, base)
    base = jnp.where(places == where_zero, 0, base)
    return base.reshape(PP, TOKENS).astype(jnp.int32)


def with_ends(array, key, low, high):
    shape = array.shape
    place = [jax.random.randint(jax.random.fold_in(key, axis), (), 0, shape[axis]) for axis in range(len(shape))]
    array = array.at[tuple(place)].set(low)
    longest = shape.index(max(shape))
    place[longest] = (place[longest] + 1) % shape[longest]
    return array.at[tuple(place)].set(high)


def raised(entries, own_key, source, target, parts, factor):
    def block_of(dim):
        return (jnp.arange(entries.shape[dim]) // (entries.shape[dim] // parts)).reshape((-1,) + (1,) * (entries.ndim - 1 - dim))

    one_side = jax.random.permutation(own_key, parts)[block_of(target)]
    second = (block_of(target) + parts // 2) % parts
    return jnp.where((block_of(source) == one_side) | (block_of(source) == second), factor * entries, entries)


def block_levels(key, extent, cuts, smallest, high):
    def one(dim, blocks):
        steps = jax.random.uniform(jax.random.fold_in(jax.random.fold_in(key, 6), dim), (blocks,), jnp.float32, smallest / len(cuts), high / len(cuts))
        return jnp.repeat(jnp.exp(steps), extent[dim] // blocks).reshape((-1,) + (1,) * (len(extent) - dim - 1))

    gain = one(*cuts[0])
    for cut in cuts[1:]:
        gain = gain * one(*cut)
    return gain


def gaussian(stream_key, extent, spread, reach, cuts=(), kind=jnp.bfloat16):
    level = block_levels(stream_key, extent, cuts, -0.22, 0.18) if cuts else 1.0
    drawn = jax.random.normal(stream_key, extent, jnp.float32) * spread * level
    return jnp.minimum(jnp.maximum(drawn, -reach), reach).astype(kind)


def bell_draw_with(key, shape, scale, limit, split, heavy, held_as=jnp.bfloat16):
    values = scale * jax.random.normal(key, shape, jnp.float32)
    if split:
        values = values * block_levels(key, shape, split, -0.22, 0.18)
    return jnp.clip(raised(values, jax.random.fold_in(key, 3), *heavy), -limit, limit).astype(held_as)


def setup_inputs(seed: int = 0) -> dict:
    keys = jax.random.split(jax.random.key(seed), 9)
    return {
        "tokens": bell_draw_with(keys[0], (TOKENS, D), 1.0, 16.0, ((0, 64), (1, 8)), (0, 1, 64, 4.0)),
        "first_weight": gaussian(keys[1], (D, D), D ** -0.5, 0.1875, ((1, 8),)),
        "second_weight": gaussian(keys[2], (D, D), D ** -0.5, 0.1875, ((1, 8),)),
        "head_weight": gaussian(keys[3], (COLS, D), D ** -0.5, 0.1875, ((0, 8),)),
        "targets": gaussian(keys[4], (COLS, TOKENS), 1.0, 6.0, ((0, 8), (1, 64)), jnp.float32),
        "land_mask": draw_land_mask(jax.random.fold_in(keys[8], 71), 0),
        "variable_kind": with_ends(jax.random.randint(keys[6], (V,), 0, 3), jax.random.fold_in(keys[6], 1), 0, 2).astype(jnp.int32),
        "loss_scale": jnp.clip(jnp.exp(jax.random.uniform(keys[7], (), jnp.float32, math.log(2523136), math.log(20185088))), 2523136, 20185088),
    }


def slope(z):
    cdf = 0.5 * (1.0 + lax.erf(z / math.sqrt(2.0)))
    return cdf + z * jnp.exp(-0.5 * z * z) / math.sqrt(2.0 * math.pi)

def reference(tokens, first_weight, second_weight, head_weight, targets, land_mask, variable_kind, loss_scale):
    pre_one = jnp.dot(tokens, first_weight, preferred_element_type=jnp.float32)
    hidden_one = jax.nn.gelu(pre_one, approximate=False).astype(jnp.bfloat16)
    pre_two = jnp.dot(hidden_one, second_weight, preferred_element_type=jnp.float32)
    hidden_two = jax.nn.gelu(pre_two, approximate=False).astype(jnp.bfloat16)
    predicted = jnp.dot(head_weight, hidden_two.T, preferred_element_type=jnp.float32)
    position = jnp.arange(TOKENS, dtype=jnp.int32)
    cell = jnp.arange(PP, dtype=jnp.int32)
    lat_row = 2 * (position // LONP)[None, :] + (cell // 2)[:, None]
    nlat = 2 * TOKENS // LONP
    cell_weight = jnp.cos(math.pi / 2.0 * (lat_row.astype(jnp.float32) + 0.5) / nlat)
    land = land_mask.astype(jnp.float32)
    kind = variable_kind[:, None, None]
    valid = jnp.where(kind == 0, 1.0, jnp.where(kind == 1, land[None], 1.0 - land[None])).astype(jnp.float32)
    masked = cell_weight[None] * valid
    error = predicted.reshape(V, PP, TOKENS) - targets.reshape(V, PP, TOKENS)
    weight_sum = lax.optimization_barrier(jnp.sum(masked, axis=(1, 2)))
    error_sum = lax.optimization_barrier(jnp.sum(masked * error * error, axis=(1, 2)))
    root = jnp.sqrt(error_sum / weight_sum + 1e-06)
    loss = jnp.mean(root)
    coef = loss_scale / (V * root * weight_sum)
    grad_pred = (coef[:, None, None] * masked * error).reshape(COLS, TOKENS).astype(jnp.bfloat16)
    head_grad = jnp.dot(grad_pred, hidden_two, preferred_element_type=jnp.float32)
    back_two = jnp.dot(grad_pred.T, head_weight, preferred_element_type=jnp.float32)
    grad_two = (back_two * slope(pre_two)).astype(jnp.bfloat16)
    second_grad = jnp.dot(hidden_one.T, grad_two, preferred_element_type=jnp.float32)
    back_one = jnp.dot(grad_two, second_weight.T, preferred_element_type=jnp.float32)
    grad_one = (back_one * slope(pre_one)).astype(jnp.bfloat16)
    first_grad = jnp.dot(tokens.T, grad_one, preferred_element_type=jnp.float32)
    token_grad = jnp.dot(grad_one, first_weight.T, preferred_element_type=jnp.float32)
    return (loss, token_grad, first_grad, second_grad, head_grad)
```

```python
import math

import jax
import jax.numpy as jnp
from jax import lax
from jax.experimental import pallas as pl
from jax.experimental.pallas import tpu as pltpu
from jax.sharding import Mesh
from jax.sharding import PartitionSpec as P

V = 88
PP = 4
LONP = 224
D = 1024
OWN = 112
HEAD = 48
COLS = 8 * HEAD
BF = jnp.bfloat16
F32 = jnp.float32
SPACE = ("z", "y")
TENSOR = ("x", "core")
OFFS = (0, 3, 1, 2)


def dot(a, b, da, db):
    return lax.dot_general(a, b, (((da,), (db,)), ((), ())), preferred_element_type=F32)


def lanes(j):
    return pl.ds(pl.multiple_of(j * 128, 128), 128)


def call(body, name, outs, args, smem=(), scratch=(), flops=0, vmem=56):
    specs = [
        pl.BlockSpec(memory_space=pltpu.SMEM if i in smem else pltpu.VMEM) for i in range(len(args))
    ]
    return pl.pallas_call(
        body,
        name=name,
        out_shape=tuple(jax.ShapeDtypeStruct(s, t) for s, t in outs),
        in_specs=specs,
        out_specs=tuple(pl.BlockSpec(memory_space=pltpu.VMEM) for _ in outs),
        scratch_shapes=list(scratch),
        compiler_params=pltpu.CompilerParams(vmem_limit_bytes=vmem * 2**20),
        cost_estimate=pl.CostEstimate(flops=flops, bytes_accessed=4 * 2**20, transcendentals=0),
    )(*args)


def prep_body(head, second, targets, kinds, packed, tgt):
    packed[:D, :] = second[...]
    for i in range(8):
        packed[D + HEAD * i : D + HEAD * (i + 1), :] = head[:, 128 * i : 128 * (i + 1)]
        tgt[i, :, :OWN] = targets[:, OWN * i : OWN * (i + 1)]
        tgt[i, :, OWN:] = jnp.broadcast_to(kinds[...], (HEAD, 128 - OWN))


def gelu_parts(z):
    cdf = 0.5 * (1.0 + lax.erf(z * (1.0 / math.sqrt(2.0))))
    return z * cdf, cdf + z * jnp.exp(-0.5 * z * z) * (1.0 / math.sqrt(2.0 * math.pi))


def pairs(near, far):
    for a, ref in enumerate((near, far)):
        for s in (0, 2):
            yield ref, s, 4 * a + s


def forward_body(
    idx, tok, w1n, w1f, w2n, w2f, tgt, land, weights,
    xh, slope1, slope2, hidden2, me, sums, head, pre,
):
    for j in range(8):
        xh[:, 128 * j : 128 * (j + 1)] = tok[j]
    for a, ref in enumerate((w2n, w2f)):
        for s in range(4):
            rows = pl.ds(pl.multiple_of(idx[4 * a + s] * HEAD, HEAD), HEAD)
            for i in range(8):
                head[rows, 128 * i : 128 * (i + 1)] = ref[s, D + HEAD * i : D + HEAD * (i + 1), :]

    def layer(value, near, far):
        for ref, s, at in pairs(near, far):
            both = jnp.concatenate([ref[s, :D, :], ref[s + 1, :D, :]], axis=1)
            z = dot(value, both, 1, 0)
            pre[:, lanes(idx[at])] = z[:, :128]
            pre[:, lanes(idx[at + 1])] = z[:, 128:]

    layer(xh[:, :D], w1n, w1f)
    hidden, slope = gelu_parts(pre[...])
    xh[:, D:] = hidden.astype(BF)
    slope1[...] = slope
    layer(xh[:, D:], w2n, w2f)
    hidden, slope = gelu_parts(pre[...])
    hidden2[...] = hidden.astype(BF)
    slope2[...] = slope
    predicted = dot(hidden2[...], head[...], 1, 1)
    flipped = tgt[...].reshape(COLS, 128).T
    kind = flipped[OWN : OWN + 1, :]
    column = lax.broadcasted_iota(jnp.int32, (8, COLS), 1)
    picks = (column % PP == lax.broadcasted_iota(jnp.int32, (8, COLS), 0)).astype(BF)
    on_land = dot(land[...], picks, 0, 0)[:OWN, :]
    valid = jnp.where(kind == 0.0, 1.0, jnp.where(kind == 1.0, on_land, 1.0 - on_land))
    masked = weights[...] * valid
    error = predicted - flipped[:OWN, :]
    product = masked * error
    me[...] = product
    sums[0:1, :] = jnp.sum(product * error, axis=0, keepdims=True)
    sums[1:2, :] = jnp.sum(masked, axis=0, keepdims=True)


def head_body(idx, me, hidden2, keep, send, full):
    full[...] = dot(me[...].astype(BF), hidden2[...], 0, 0)
    core = idx[8]
    for k in range(4):
        for ref, c in ((keep, core), (send, 1 - core)):
            rows = pl.ds(pl.multiple_of((2 * k + c) * HEAD, HEAD), HEAD)
            ref[k] = full[rows, :].astype(BF)


def pair_body(idx, keep, came, own, up, down, across):
    x = idx[9]
    for ref, off in ((own, 0), (up, 1), (down, 3), (across, 2)):
        k = lax.rem(x + off, 4)
        ref[...] = (keep[k].astype(F32) + came[k].astype(F32)).astype(BF)


def over_cells(v):
    column = lax.broadcasted_iota(jnp.int32, v.shape, 1)
    n = v.shape[1]
    for step in (1, 2):
        ahead = pltpu.roll(v, n - step, 1)
        behind = pltpu.roll(v, step, 1)
        v = v + jnp.where((column // step) % 2 == 0, ahead, behind)
    return v


def backward_body(
    idx, scale, sums, me, slope1, slope2, head, w2n, w2f, joined, grad1, coefs, loss, g2
):
    total = over_cells(jnp.sum(sums[...], axis=0))
    column = lax.broadcasted_iota(jnp.int32, (1, COLS), 1)
    real = column % HEAD < V * PP // 8
    weight = jnp.where(real, total[1:2, :], 1.0)
    root = jnp.sqrt(total[0:1, :] / weight + 1e-06)
    loss[...] = jnp.sum(jnp.where(real, root, 0.0), axis=1, keepdims=True) / (V * PP)
    coef = jnp.where(real, scale[0] / (V * root * weight), 0.0)
    coefs[...] = coef
    grad_pred = (coef * me[...]).astype(BF)
    g2[...] = (dot(grad_pred, head[...], 1, 0) * slope2[...]).astype(BF)
    back = jnp.zeros((OWN, D), F32)
    for ref, s, at in pairs(w2n, w2f):
        both = jnp.concatenate([ref[s, :D, :], ref[s + 1, :D, :]], axis=1)
        left = jnp.concatenate([g2[:, lanes(idx[at])], g2[:, lanes(idx[at + 1])]], axis=1)
        back += dot(left, both, 1, 1)
    grad1[...] = (back * slope1[...]).astype(BF)
    for j in range(8):
        joined[j, :, :128] = g2[:, 128 * j : 128 * (j + 1)]
        joined[j, :, 128:] = grad1[:, 128 * j : 128 * (j + 1)]


def token_body(idx, grad1, w1n, w1f, out):
    grad = jnp.zeros((OWN, D), F32)
    for ref, s, at in pairs(w1n, w1f):
        both = jnp.concatenate([ref[s], ref[s + 1]], axis=1)
        left = jnp.concatenate([grad1[:, lanes(idx[at])], grad1[:, lanes(idx[at + 1])]], axis=1)
        grad += dot(left, both, 1, 1)
    for j in range(8):
        out[j] = grad[:, 128 * j : 128 * (j + 1)]


def weight_body(idx, xhn, xhf, joined, own, a, b, c, out, order):
    for at in range(8):
        order[OWN * at : OWN * (at + 1), :] = joined[idx[at]]
    half = 4 * OWN
    near, far = xhn[...].reshape(half, 2 * D), xhf[...].reshape(half, 2 * D)
    for to, at in ((0, D), (128, 0)):
        grad = dot(order[:half, to : to + 128], near[:, at : at + D], 0, 0)
        grad += dot(order[half:, to : to + 128], far[:, at : at + D], 0, 0)
        out[:, :, to : to + 128] = grad.T.astype(BF).reshape(64, 16, 128)
    part = own[...].astype(F32) + a[...].astype(F32) + b[...].astype(F32) + c[...].astype(F32)
    part = jnp.concatenate([part, jnp.zeros((128 - HEAD, D), F32)], axis=0)
    out[:, :, 256:] = part.T.astype(BF).reshape(64, 16, 128)


def shift(v, by):
    return lax.ppermute(v, "x", [(i, (i + by) % 4) for i in range(4)])


def flip(v):
    return lax.ppermute(v, "core", [(0, 1), (1, 0)])


def per_device(
    tokens, first_weight, second_weight, head_weight, targets, land_mask, variable_kind, loss_scale
):
    x, core = lax.axis_index("x"), lax.axis_index("core")
    mine = lax.axis_index(TENSOR)
    places = [2 * ((x + off) % 4) + c for c in (core, 1 - core) for off in OFFS]
    idx = jnp.stack([*places, core, x]).astype(jnp.int32)

    padded_head = jnp.pad(head_weight, ((0, HEAD - 44), (0, 0)))
    padded_targets = jnp.pad(targets, ((0, HEAD - 44), (0, 0)))
    kinds = jnp.pad(jnp.repeat(variable_kind, PP), (0, HEAD - 44)).astype(F32)[:, None]
    packed, tgt = call(
        prep_body, "prep", [((D + COLS, 128), BF), ((8, HEAD, 128), F32)],
        [padded_head, second_weight, padded_targets, kinds],
    )

    own_tokens = lax.all_to_all(tokens.reshape(8, OWN, 128), TENSOR, 0, 0, tiled=True)
    w1_m1, w1_p1 = shift(first_weight, 1), shift(first_weight, 3)
    w2_m1, w2_p1 = shift(packed, 1), shift(packed, 3)
    w1_p2, w2_p2 = shift(w1_m1, 1), shift(w2_p1, 3)
    w1n = jnp.stack([first_weight, w1_m1, w1_p1, w1_p2])
    w2n = jnp.stack([packed, w2_m1, w2_p1, w2_p2])
    w1f, w2f = flip(w1n), flip(w2n)
    tgt = lax.all_to_all(tgt, TENSOR, 0, 0, tiled=True)

    land = lax.dynamic_slice(land_mask, (0, mine * OWN), (PP, OWN))
    land = jnp.pad(land.astype(BF), ((0, 8 - PP), (0, 128 - OWN)))
    space = lax.axis_index(SPACE)
    patch_row = (space * 8 * OWN + mine * OWN) // LONP
    nlat = 2 * (64 * 8 * OWN // LONP)
    col = jnp.arange(COLS, dtype=jnp.int32)
    lat_row = 2 * patch_row + (col % PP) // 2
    weights = jnp.cos(math.pi / 2.0 * (lat_row.astype(F32) + 0.5) / nlat)
    weights = jnp.where(col % HEAD < 44, weights, 0.0)[None, :]

    xh, slope1, slope2, hidden2, me, sums, head = call(
        forward_body, "forward",
        [((OWN, 2 * D), BF), ((OWN, D), F32), ((OWN, D), F32), ((OWN, D), BF), ((OWN, COLS), F32),
         ((2, COLS), F32), ((COLS, D), BF)],
        [idx, own_tokens, w1n, w1f, w2n, w2f, tgt, land, weights],
        smem=(0,), scratch=[pltpu.VMEM((OWN, D), F32)], flops=10**9,
    )

    sums = jnp.sum(
        lax.all_to_all(jnp.broadcast_to(sums, (8, 2, COLS)), TENSOR, 0, 0, tiled=True), axis=0
    )
    sums = lax.all_to_all(jnp.broadcast_to(sums, (64, 2, COLS)), SPACE, 0, 0, tiled=True)

    xhn = jnp.stack([xh, shift(xh, 1), shift(xh, 3), shift(xh, 2)])
    xhf = flip(xhn)
    keep, send = call(
        head_body, "head_part", [((4, HEAD, D), BF)] * 2, [idx, me, hidden2],
        smem=(0,), scratch=[pltpu.VMEM((COLS, D), F32)], flops=10**8,
    )
    own, up, down, across = call(
        pair_body, "pair", [((HEAD, D), BF)] * 4, [idx, keep, flip(send)], smem=(0,)
    )
    head_parts = [own, shift(up, 1), shift(down, 3), shift(across, 2)]

    joined, grad1, coefs, loss = call(
        backward_body, "backward",
        [((8, OWN, 256), BF), ((OWN, D), BF), ((1, COLS), F32), ((1, 1), F32)],
        [idx, loss_scale.reshape(1), sums, me, slope1, slope2, head, w2n, w2f],
        smem=(0, 1), scratch=[pltpu.VMEM((OWN, D), BF)], flops=5 * 10**8,
    )
    joined = lax.all_to_all(joined, TENSOR, 0, 0, tiled=True)
    (token_grad,) = call(
        token_body, "token", [((8, OWN, 128), F32)], [idx, grad1, w1n, w1f], smem=(0,), flops=3 * 10**8
    )
    (out,) = call(
        weight_body, "weight", [((64, 16, 384), BF)], [idx, xhn, xhf, joined, *head_parts],
        smem=(0,), scratch=[pltpu.VMEM((8 * OWN, 256), BF)], flops=5 * 10**8,
    )
    out = lax.all_to_all(out, SPACE, 0, 0, tiled=True)
    token_grad = lax.all_to_all(token_grad, TENSOR, 0, 0, tiled=True).reshape(8 * OWN, 128)
    out = jnp.sum(out.astype(F32), axis=0)
    local = lax.dynamic_slice(coefs, (0, mine * HEAD), (1, 44))
    head_grad = (out[:, 256:300] * local).T
    return loss.reshape(()), token_grad, out[:, 128:256], out[:, :128], head_grad


def solution(mesh):
    inner = Mesh(mesh.devices.reshape(8, 8, 4, 2), ("z", "y", "x", "core"))
    return jax.shard_map(
        per_device,
        mesh=inner,
        in_specs=(
            P(SPACE, TENSOR),
            P(None, TENSOR),
            P(None, TENSOR),
            P(TENSOR, None),
            P(TENSOR, SPACE),
            P(None, SPACE),
            P(TENSOR),
            P(),
        ),
        out_specs=(
            P(),
            P(SPACE, TENSOR),
            P(SPACE, TENSOR),
            P(SPACE, TENSOR),
            P(TENSOR, SPACE),
        ),
        check_vma=False,
    )
```

```python
import math

import jax
import jax.numpy as jnp
from jax import lax
from jax.experimental import pallas as pl
from jax.experimental.pallas import tpu as pltpu
from jax.sharding import Mesh
from jax.sharding import PartitionSpec as P

V = 88
PP = 4
LONP = 224
D = 1024
OWN = 112
HEAD = 48
WIDE = 64
COLS = 8 * HEAD
BF = jnp.bfloat16
F32 = jnp.float32
SPACE = ("z", "y")
TENSOR = ("x", "core")
OFFS = (0, 3, 1, 2)


def dot(a, b, da, db):
    return lax.dot_general(a, b, (((da,), (db,)), ((), ())), preferred_element_type=F32)


def lanes(j):
    return pl.ds(pl.multiple_of(j * 128, 128), 128)


def call(body, name, outs, args, smem=(), scratch=(), flops=0, vmem=56):
    specs = [
        pl.BlockSpec(memory_space=pltpu.SMEM if i in smem else pltpu.VMEM) for i in range(len(args))
    ]
    return pl.pallas_call(
        body,
        name=name,
        out_shape=tuple(jax.ShapeDtypeStruct(s, t) for s, t in outs),
        in_specs=specs,
        out_specs=tuple(pl.BlockSpec(memory_space=pltpu.VMEM) for _ in outs),
        scratch_shapes=list(scratch),
        compiler_params=pltpu.CompilerParams(vmem_limit_bytes=vmem * 2**20),
        cost_estimate=pl.CostEstimate(flops=flops, bytes_accessed=4 * 2**20, transcendentals=0),
    )(*args)


def prep_body(kinds, tokens, targets, out):
    real = V * PP // 8
    row = lax.broadcasted_iota(jnp.int32, (HEAD, 128 - OWN), 0)
    kind = jnp.zeros(row.shape, F32)
    for v in range(V // 8):
        kind = jnp.where(row // PP == v, kinds[v].astype(F32), kind)
    for i in range(8):
        out[i, :OWN, :] = tokens[OWN * i : OWN * (i + 1), :]
        rest = jnp.concatenate([targets[:, OWN * i : OWN * (i + 1)], kind[:real]], axis=1)
        rest = jnp.concatenate([rest, jnp.zeros((HEAD - real, 128), F32)], axis=0)
        for piece in range(3):
            at = OWN + HEAD * piece
            part = rest.astype(BF)
            out[i, at : at + HEAD, :] = part
            rest = rest - part.astype(F32)


def gelu_parts(z):
    cdf = 0.5 * (1.0 + lax.erf(z * (1.0 / math.sqrt(2.0))))
    return z * cdf, cdf + z * jnp.exp(-0.5 * z * z) * (1.0 / math.sqrt(2.0 * math.pi))


def pairs(near, far):
    for a, ref in enumerate((near, far)):
        for s in (0, 2):
            yield ref, s, 4 * a + s


def forward_body(
    idx, given, w1n, w1f, w2n, w2f, heads, land, weights,
    hidden1, slope1, slope2, hidden2, me, sums, head, own, pre,
):
    for j in range(8):
        own[:, 128 * j : 128 * (j + 1)] = given[j, :OWN, :]
        head[HEAD * j : HEAD * (j + 1), :] = heads[WIDE * j : WIDE * j + HEAD, :]

    def layer(value, near, far):
        for ref, s, at in pairs(near, far):
            both = jnp.concatenate([ref[s], ref[s + 1]], axis=1)
            z = dot(value, both, 1, 0)
            pre[:, lanes(idx[at])] = z[:, :128]
            pre[:, lanes(idx[at + 1])] = z[:, 128:]

    layer(own[...], w1n, w1f)
    hidden, slope = gelu_parts(pre[...])
    hidden1[...] = hidden.astype(BF)
    slope1[...] = slope
    layer(hidden1[...], w2n, w2f)
    hidden, slope = gelu_parts(pre[...])
    hidden2[...] = hidden.astype(BF)
    slope2[...] = slope
    predicted = dot(hidden2[...], head[...], 1, 1)
    pieces = [given[:, OWN + HEAD * p : OWN + HEAD * (p + 1), :].astype(F32) for p in range(3)]
    flipped = (pieces[0] + (pieces[1] + pieces[2])).reshape(COLS, 128).T
    kind = flipped[OWN : OWN + 1, :]
    column = lax.broadcasted_iota(jnp.int32, (8, COLS), 1)
    picks = (column % PP == lax.broadcasted_iota(jnp.int32, (8, COLS), 0)).astype(BF)
    on_land = dot(land[...], picks, 0, 0)[:OWN, :]
    valid = jnp.where(kind == 0.0, 1.0, jnp.where(kind == 1.0, on_land, 1.0 - on_land))
    masked = weights[...] * valid
    error = predicted - flipped[:OWN, :]
    product = masked * error
    me[...] = product
    sums[0:1, :] = jnp.sum(product * error, axis=0, keepdims=True)
    sums[1:2, :] = jnp.sum(masked, axis=0, keepdims=True)


def head_body(idx, me, hidden2, keep, send, full):
    full[...] = dot(me[...].astype(BF), hidden2[...], 0, 0)
    core = idx[8]
    for k in range(4):
        for ref, c in ((keep, core), (send, 1 - core)):
            rows = pl.ds(pl.multiple_of((2 * k + c) * HEAD, HEAD), HEAD)
            ref[k] = full[rows, :].astype(BF)


def pair_body(idx, keep, came, own, up, down, across):
    x = idx[9]
    for ref, off in ((own, 0), (up, 1), (down, 3), (across, 2)):
        k = lax.rem(x + off, 4)
        ref[...] = (keep[k].astype(F32) + came[k].astype(F32)).astype(BF)


def over_cells(v):
    column = lax.broadcasted_iota(jnp.int32, v.shape, 1)
    n = v.shape[1]
    for step in (1, 2):
        ahead = pltpu.roll(v, n - step, 1)
        behind = pltpu.roll(v, step, 1)
        v = v + jnp.where((column // step) % 2 == 0, ahead, behind)
    return v


def backward_body(
    idx, scale, sums, me, slope1, slope2, head, w2n, w2f, joined, grad1, coefs, loss, g2
):
    total = over_cells(jnp.sum(sums[...], axis=0))
    column = lax.broadcasted_iota(jnp.int32, (1, COLS), 1)
    real = column % HEAD < V * PP // 8
    weight = jnp.where(real, total[1:2, :], 1.0)
    root = jnp.sqrt(total[0:1, :] / weight + 1e-06)
    loss[...] = jnp.sum(jnp.where(real, root, 0.0), axis=1, keepdims=True) / (V * PP)
    coef = jnp.where(real, scale[0] / (V * root * weight), 0.0)
    coefs[...] = coef
    grad_pred = (coef * me[...]).astype(BF)
    g2[...] = (dot(grad_pred, head[...], 1, 0) * slope2[...]).astype(BF)
    back = jnp.zeros((OWN, D), F32)
    for ref, s, at in pairs(w2n, w2f):
        both = jnp.concatenate([ref[s], ref[s + 1]], axis=1)
        left = jnp.concatenate([g2[:, lanes(idx[at])], g2[:, lanes(idx[at + 1])]], axis=1)
        back += dot(left, both, 1, 1)
    grad1[...] = (back * slope1[...]).astype(BF)
    for j in range(8):
        joined[j, :, :128] = g2[:, 128 * j : 128 * (j + 1)]
        joined[j, :, 128:] = grad1[:, 128 * j : 128 * (j + 1)]


def token_body(idx, grad1, w1n, w1f, out):
    rows = lanes(idx[10])
    grad = jnp.zeros((8 * OWN, 128), F32)
    for ref, s, at in pairs(w1n, w1f):
        both = jnp.concatenate([ref[s, rows, :], ref[s + 1, rows, :]], axis=1)
        left = jnp.concatenate([grad1[:, lanes(idx[at])], grad1[:, lanes(idx[at + 1])]], axis=1)
        grad += dot(left, both, 1, 1)
    out[...] = grad


def weight_body(hidden1, tokens, joined, own, a, b, c, out):
    grads = joined[...].reshape(8 * OWN, 256)
    for to, value in ((0, hidden1), (128, tokens)):
        grad = dot(grads[:, to : to + 128], value[...], 0, 0)
        out[:, :, to : to + 128] = grad.T.astype(BF).reshape(64, 16, 128)
    part = own[...].astype(F32) + a[...].astype(F32) + b[...].astype(F32) + c[...].astype(F32)
    part = jnp.concatenate([part, jnp.zeros((128 - HEAD, D), F32)], axis=0)
    out[:, :, 256:] = part.T.astype(BF).reshape(64, 16, 128)


def shift(v, by):
    return lax.ppermute(v, "x", [(i, (i + by) % 4) for i in range(4)])


def flip(v):
    return lax.ppermute(v, "core", [(0, 1), (1, 0)])


def per_device(
    tokens, first_weight, second_weight, head_weight, targets, land_mask, variable_kind, loss_scale
):
    x, core = lax.axis_index("x"), lax.axis_index("core")
    mine = lax.axis_index(TENSOR)
    places = [2 * ((x + off) % 4) + c for c in (core, 1 - core) for off in OFFS]
    idx = jnp.stack([*places, core, x, mine]).astype(jnp.int32)

    full_tokens = lax.all_gather(tokens, TENSOR, axis=1, tiled=True)
    wide = jnp.pad(head_weight, ((0, WIDE - V * PP // 8), (0, 0)))
    heads = lax.all_gather(wide, TENSOR, axis=0, tiled=True)
    (given,) = call(
        prep_body, "prep", [((8, OWN + 3 * HEAD, 128), BF)], [variable_kind, tokens, targets],
        smem=(0,),
    )
    given = lax.all_to_all(given, TENSOR, 0, 0, tiled=True)

    w1_m1, w1_p1 = shift(first_weight, 1), shift(first_weight, 3)
    w2_m1, w2_p1 = shift(second_weight, 1), shift(second_weight, 3)
    w1_m1, w2_p1, given = lax.optimization_barrier((w1_m1, w2_p1, given))
    w1_p2, w2_p2 = shift(w1_m1, 1), shift(w2_p1, 3)
    w1n = jnp.stack([first_weight, w1_m1, w1_p1, w1_p2])
    w2n = jnp.stack([second_weight, w2_m1, w2_p1, w2_p2])
    w1f = flip(w1n)
    w2f = flip(w2n)

    land = lax.dynamic_slice(land_mask, (0, mine * OWN), (PP, OWN))
    land = jnp.pad(land.astype(BF), ((0, 8 - PP), (0, 128 - OWN)))
    space = lax.axis_index(SPACE)
    patch_row = (space * 8 * OWN + mine * OWN) // LONP
    nlat = 2 * (64 * 8 * OWN // LONP)
    col = jnp.arange(COLS, dtype=jnp.int32)
    lat_row = 2 * patch_row + (col % PP) // 2
    weights = jnp.cos(math.pi / 2.0 * (lat_row.astype(F32) + 0.5) / nlat)
    weights = jnp.where(col % HEAD < 44, weights, 0.0)[None, :]

    hidden1, slope1, slope2, hidden2, me, sums, head = call(
        forward_body, "forward",
        [((OWN, D), BF), ((OWN, D), F32), ((OWN, D), F32), ((OWN, D), BF), ((OWN, COLS), F32),
         ((2, COLS), F32), ((COLS, D), BF)],
        [idx, given, w1n, w1f, w2n, w2f, heads, land, weights],
        smem=(0,), scratch=[pltpu.VMEM((OWN, D), BF), pltpu.VMEM((OWN, D), F32)], flops=10**9,
    )
    full_hidden1 = lax.all_gather(hidden1, TENSOR, axis=0, tiled=True)

    sums = jnp.sum(
        lax.all_to_all(jnp.broadcast_to(sums, (8, 2, COLS)), TENSOR, 0, 0, tiled=True), axis=0
    )
    sums, me, hidden2 = lax.optimization_barrier((sums, me, hidden2))
    sums = lax.all_to_all(jnp.broadcast_to(sums, (64, 2, COLS)), SPACE, 0, 0, tiled=True)

    keep, send = call(
        head_body, "head_part", [((4, HEAD, D), BF)] * 2, [idx, me, hidden2],
        smem=(0,), scratch=[pltpu.VMEM((COLS, D), F32)], flops=10**8,
    )
    own, up, down, across = call(
        pair_body, "pair", [((HEAD, D), BF)] * 4, [idx, keep, flip(send)], smem=(0,)
    )
    head_parts = [own, shift(up, 1), shift(down, 3), shift(across, 2)]
    sums, head_parts = lax.optimization_barrier((sums, head_parts))

    joined, grad1, coefs, loss = call(
        backward_body, "backward",
        [((8, OWN, 256), BF), ((OWN, D), BF), ((1, COLS), F32), ((1, 1), F32)],
        [idx, loss_scale.reshape(1), sums, me, slope1, slope2, head, w2n, w2f],
        smem=(0, 1), scratch=[pltpu.VMEM((OWN, D), BF)], flops=5 * 10**8,
    )
    joined = lax.all_to_all(joined, TENSOR, 0, 0, tiled=True)
    full_grad1 = lax.all_gather(grad1, TENSOR, axis=0, tiled=True)
    (out,) = call(
        weight_body, "weight", [((64, 16, 384), BF)],
        [full_hidden1, full_tokens, joined, *head_parts], flops=5 * 10**8,
    )
    out = lax.all_to_all(out, SPACE, 0, 0, tiled=True)
    (token_grad,) = call(
        token_body, "token", [((8 * OWN, 128), F32)], [idx, full_grad1, w1n, w1f],
        smem=(0,), flops=3 * 10**8,
    )
    out = jnp.sum(out.astype(F32), axis=0)
    local = lax.dynamic_slice(coefs, (0, mine * HEAD), (1, 44))
    head_grad = (out[:, 256:300] * local).T
    return loss.reshape(()), token_grad, out[:, 128:256], out[:, :128], head_grad


def solution(mesh):
    inner = Mesh(mesh.devices.reshape(8, 8, 4, 2), ("z", "y", "x", "core"))
    return jax.shard_map(
        per_device,
        mesh=inner,
        in_specs=(
            P(SPACE, TENSOR),
            P(None, TENSOR),
            P(None, TENSOR),
            P(TENSOR, None),
            P(TENSOR, SPACE),
            P(None, SPACE),
            P(TENSOR),
            P(),
        ),
        out_specs=(
            P(),
            P(SPACE, TENSOR),
            P(SPACE, TENSOR),
            P(SPACE, TENSOR),
            P(TENSOR, SPACE),
        ),
        check_vma=False,
    )
```

```python
import math

import jax
import jax.numpy as jnp
from jax import lax
from jax.experimental import pallas as pl
from jax.experimental.pallas import tpu as pltpu
from jax.sharding import Mesh
from jax.sharding import PartitionSpec as P

V = 88
PP = 4
LONP = 224
D = 1024
OWN = 112
HEAD = 48
COLS = 8 * HEAD
BF = jnp.bfloat16
F32 = jnp.float32
SPACE = ("z", "ya", "yb")
NEAR = ("yb", "x", "core")
FAR = ("z", "ya")
TENSOR = ("x", "core")
OFFS = (0, 3, 1, 2)


def dot(a, b, da, db):
    return lax.dot_general(a, b, (((da,), (db,)), ((), ())), preferred_element_type=F32)


def lanes(j):
    return pl.ds(pl.multiple_of(j * 128, 128), 128)


def call(body, name, outs, args, smem=(), scratch=(), flops=0, vmem=56):
    specs = [
        pl.BlockSpec(memory_space=pltpu.SMEM if i in smem else pltpu.VMEM) for i in range(len(args))
    ]
    return pl.pallas_call(
        body,
        name=name,
        out_shape=tuple(jax.ShapeDtypeStruct(s, t) for s, t in outs),
        in_specs=specs,
        out_specs=tuple(pl.BlockSpec(memory_space=pltpu.VMEM) for _ in outs),
        scratch_shapes=list(scratch),
        compiler_params=pltpu.CompilerParams(vmem_limit_bytes=vmem * 2**20),
        cost_estimate=pl.CostEstimate(flops=flops, bytes_accessed=4 * 2**20, transcendentals=0),
    )(*args)


def prep_body(kinds, tokens, targets, second, head, out, packed):
    real = V * PP // 8
    row = lax.broadcasted_iota(jnp.int32, (HEAD, 128 - OWN), 0)
    kind = jnp.zeros(row.shape, F32)
    for v in range(V // 8):
        kind = jnp.where(row // PP == v, kinds[v].astype(F32), kind)
    blank = jnp.zeros((HEAD - real, 128), F32)
    packed[:D, :] = second[...]
    for i in range(8):
        out[i, :OWN, :] = tokens[OWN * i : OWN * (i + 1), :]
        rest = jnp.concatenate([targets[:, OWN * i : OWN * (i + 1)], kind[:real]], axis=1)
        rest = jnp.concatenate([rest, blank], axis=0)
        for piece in range(3):
            at = OWN + HEAD * piece
            part = rest.astype(BF)
            out[i, at : at + HEAD, :] = part
            rest = rest - part.astype(F32)
        rows = jnp.concatenate([head[:, 128 * i : 128 * (i + 1)].astype(F32), blank], axis=0)
        packed[D + HEAD * i : D + HEAD * (i + 1), :] = rows.astype(BF)


def gelu_parts(z):
    cdf = 0.5 * (1.0 + lax.erf(z * (1.0 / math.sqrt(2.0))))
    return z * cdf, cdf + z * jnp.exp(-0.5 * z * z) * (1.0 / math.sqrt(2.0 * math.pi))


def block(refs, a, s, rows):
    three, last = refs[2 * a], refs[2 * a + 1]
    return three[s, rows, :] if s < 3 else last[rows, :]


def pairs(refs, rows=slice(0, D)):
    for a in range(2):
        for s in (0, 2):
            both = [block(refs, a, s, rows), block(refs, a, s + 1, rows)]
            yield jnp.concatenate(both, axis=1), 4 * a + s


def layer(idx, value, refs, pre):
    for both, at in pairs(refs):
        z = dot(value, both, 1, 0)
        pre[:, lanes(idx[at])] = z[:, :128]
        pre[:, lanes(idx[at + 1])] = z[:, 128:]
    return gelu_parts(pre[...])


def back_through(idx, grad, refs, rows=slice(0, D)):
    total = None
    for both, at in pairs(refs, rows):
        left = jnp.concatenate([grad[:, lanes(idx[at])], grad[:, lanes(idx[at + 1])]], axis=1)
        term = dot(left, both, 1, 1)
        total = term if total is None else total + term
    return total


def first_body(idx, given, n3, n1, f3, f1, hidden1, slope1, own, pre):
    for j in range(8):
        own[:, 128 * j : 128 * (j + 1)] = given[j, :OWN, :]
    hidden, slope = layer(idx, own[...], (n3, n1, f3, f1), pre)
    hidden1[...] = hidden.astype(BF)
    slope1[...] = slope


def second_body(
    idx, given, hidden1, n3, n1, f3, f1, land, weights, slope2, hidden2, me, sums, head, pre
):
    refs = (n3, n1, f3, f1)
    for a in range(2):
        for s in range(4):
            rows = pl.ds(pl.multiple_of(idx[4 * a + s] * HEAD, HEAD), HEAD)
            for i in range(8):
                piece = block(refs, a, s, slice(D + HEAD * i, D + HEAD * (i + 1)))
                head[rows, 128 * i : 128 * (i + 1)] = piece
    hidden, slope = layer(idx, hidden1[...], refs, pre)
    hidden2[...] = hidden.astype(BF)
    slope2[...] = slope
    predicted = dot(hidden2[...], head[...], 1, 1)
    pieces = [given[:, OWN + HEAD * p : OWN + HEAD * (p + 1), :].astype(F32) for p in range(3)]
    flipped = (pieces[0] + (pieces[1] + pieces[2])).reshape(COLS, 128).T
    kind = flipped[OWN : OWN + 1, :]
    column = lax.broadcasted_iota(jnp.int32, (8, COLS), 1)
    picks = (column % PP == lax.broadcasted_iota(jnp.int32, (8, COLS), 0)).astype(BF)
    on_land = dot(land[...], picks, 0, 0)[:OWN, :]
    valid = jnp.where(kind == 0.0, 1.0, jnp.where(kind == 1.0, on_land, 1.0 - on_land))
    masked = weights[...] * valid
    error = predicted - flipped[:OWN, :]
    product = masked * error
    me[...] = product
    pair = [jnp.sum(product * error, axis=0, keepdims=True), jnp.sum(masked, axis=0, keepdims=True)]
    sums[...] = jnp.broadcast_to(jnp.concatenate(pair, axis=0)[None], sums.shape)


def spread_body(came, out):
    out[...] = jnp.broadcast_to(jnp.sum(came[...], axis=0, keepdims=True), out.shape)


def head_body(idx, me, hidden2, keep, send, full):
    full[...] = dot(me[...].astype(BF), hidden2[...], 0, 0)
    core = idx[8]
    for k in range(4):
        for ref, c in ((keep, core), (send, 1 - core)):
            rows = pl.ds(pl.multiple_of((2 * k + c) * HEAD, HEAD), HEAD)
            ref[k] = full[rows, :].astype(BF)


def pair_body(idx, keep, came, own, up, down, across):
    x = idx[9]
    for ref, off in ((own, 0), (up, 1), (down, 3), (across, 2)):
        k = lax.rem(x + off, 4)
        ref[...] = (keep[k].astype(F32) + came[k].astype(F32)).astype(BF)


def over_cells(v):
    column = lax.broadcasted_iota(jnp.int32, v.shape, 1)
    n = v.shape[1]
    for step in (1, 2):
        ahead = pltpu.roll(v, n - step, 1)
        behind = pltpu.roll(v, step, 1)
        v = v + jnp.where((column // step) % 2 == 0, ahead, behind)
    return v


def backward_body(
    idx, scale, sums, me, slope1, slope2, head, n3, n1, f3, f1, joined, grad1, coefs, loss, g2
):
    total = over_cells(jnp.sum(sums[...], axis=0))
    column = lax.broadcasted_iota(jnp.int32, (1, COLS), 1)
    real = column % HEAD < V * PP // 8
    weight = jnp.where(real, total[1:2, :], 1.0)
    root = jnp.sqrt(total[0:1, :] / weight + 1e-06)
    loss[...] = jnp.sum(jnp.where(real, root, 0.0), axis=1, keepdims=True) / (V * PP)
    coef = jnp.where(real, scale[0] / (V * root * weight), 0.0)
    coefs[...] = coef
    grad_pred = (coef * me[...]).astype(BF)
    g2[...] = (dot(grad_pred, head[...], 1, 0) * slope2[...]).astype(BF)
    back = back_through(idx, g2, (n3, n1, f3, f1))
    grad1[...] = (back * slope1[...]).astype(BF)
    for j in range(8):
        joined[j, :, :128] = g2[:, 128 * j : 128 * (j + 1)]
        joined[j, :, 128:] = grad1[:, 128 * j : 128 * (j + 1)]


def token_body(idx, grad1, n3, n1, f3, f1, out):
    out[...] = back_through(idx, grad1, (n3, n1, f3, f1), lanes(idx[10]))


def weight_body(hidden1, tokens, joined, own, a, b, c, out):
    grads = joined[...].reshape(8 * OWN, 256)
    second = dot(grads[:, :128], hidden1[...], 0, 0).T.reshape(64, 16, 128)
    first = dot(grads[:, 128:], tokens[...], 0, 0).T.reshape(64, 16, 128)
    part = own[...].astype(F32) + a[...].astype(F32) + b[...].astype(F32) + c[...].astype(F32)
    part = jnp.concatenate([part, jnp.zeros((128 - HEAD, D), F32)], axis=0).T
    part = part.reshape(64, 2, 8, 128)
    high = pltpu.roll(part[:, 1].reshape(512, 128), HEAD, 1).reshape(64, 8, 128)
    out[...] = jnp.concatenate([second, first, part[:, 0] + high], axis=1).astype(BF)


def shift(v, by):
    return lax.ppermute(v, "x", [(i, (i + by) % 4) for i in range(4)])


def flip(v):
    return lax.ppermute(v, "core", [(0, 1), (1, 0)])


def per_device(
    tokens, first_weight, second_weight, head_weight, targets, land_mask, variable_kind, loss_scale
):
    x, core = lax.axis_index("x"), lax.axis_index("core")
    mine = lax.axis_index(TENSOR)
    places = [2 * ((x + off) % 4) + c for c in (core, 1 - core) for off in OFFS]
    idx = jnp.stack([*places, core, x, mine]).astype(jnp.int32)

    given, packed = call(
        prep_body, "prep", [((8, OWN + 3 * HEAD, 128), BF), ((D + COLS, 128), BF)],
        [variable_kind, tokens, targets, second_weight, head_weight], smem=(0,),
    )
    given = lax.all_to_all(given, TENSOR, 0, 0, tiled=True)
    w1_m1, w1_p1 = shift(first_weight, 1), shift(first_weight, 3)
    w2_m1, w2_p1 = shift(packed, 1), shift(packed, 3)
    w1_m1, w1_p1, w2_m1, w2_p1, given = lax.optimization_barrier((w1_m1, w1_p1, w2_m1, w2_p1, given))
    w1_last, w2_last = shift(w1_m1, 1), shift(w2_p1, 3)
    w1_three = jnp.stack([first_weight, w1_m1, w1_p1])
    w2_three = jnp.stack([packed, w2_m1, w2_p1])
    w1 = (w1_three, w1_last, flip(w1_three), flip(w1_last))
    w2 = (w2_three, w2_last, flip(w2_three), flip(w2_last))
    full_tokens = lax.all_gather(tokens, TENSOR, axis=1, tiled=True)

    land = lax.dynamic_slice(land_mask, (0, mine * OWN), (PP, OWN))
    land = jnp.pad(land.astype(BF), ((0, 8 - PP), (0, 128 - OWN)))
    space = lax.axis_index(SPACE)
    patch_row = (space * 8 * OWN + mine * OWN) // LONP
    nlat = 2 * (64 * 8 * OWN // LONP)
    col = jnp.arange(COLS, dtype=jnp.int32)
    lat_row = 2 * patch_row + (col % PP) // 2
    weights = jnp.cos(math.pi / 2.0 * (lat_row.astype(F32) + 0.5) / nlat)
    weights = jnp.where(col % HEAD < 44, weights, 0.0)[None, :]

    hidden1, slope1 = call(
        first_body, "first", [((OWN, D), BF), ((OWN, D), F32)], [idx, given, *w1], smem=(0,),
        scratch=[pltpu.VMEM((OWN, D), BF), pltpu.VMEM((OWN, D), F32)], flops=3 * 10**8,
    )
    full_hidden1 = lax.all_gather(hidden1, TENSOR, axis=0, tiled=True)
    slope2, hidden2, me, sums, head = call(
        second_body, "second",
        [((OWN, D), F32), ((OWN, D), BF), ((OWN, COLS), F32), ((16, 2, COLS), F32), ((COLS, D), BF)],
        [idx, given, hidden1, *w2, land, weights],
        smem=(0,), scratch=[pltpu.VMEM((OWN, D), F32)], flops=5 * 10**8,
    )

    sums = lax.all_to_all(sums, NEAR, 0, 0, tiled=True)
    sums, me, hidden2 = lax.optimization_barrier((sums, me, hidden2))
    (sums,) = call(spread_body, "spread", [((32, 2, COLS), F32)], [sums])
    sums = lax.all_to_all(sums, FAR, 0, 0, tiled=True)

    keep, send = call(
        head_body, "head_part", [((4, HEAD, D), BF)] * 2, [idx, me, hidden2],
        smem=(0,), scratch=[pltpu.VMEM((COLS, D), F32)], flops=10**8,
    )
    own, up, down, across = call(
        pair_body, "pair", [((HEAD, D), BF)] * 4, [idx, keep, flip(send)], smem=(0,)
    )
    sums, own, up, down, across = lax.optimization_barrier((sums, own, up, down, across))
    head_parts = [own, shift(up, 1), shift(down, 3), shift(across, 2)]

    joined, grad1, coefs, loss = call(
        backward_body, "backward",
        [((8, OWN, 256), BF), ((OWN, D), BF), ((1, COLS), F32), ((1, 1), F32)],
        [idx, loss_scale.reshape(1), sums, me, slope1, slope2, head, *w2],
        smem=(0, 1), scratch=[pltpu.VMEM((OWN, D), BF)], flops=5 * 10**8,
    )
    joined = lax.all_to_all(joined, TENSOR, 0, 0, tiled=True)
    full_grad1 = lax.all_gather(grad1, TENSOR, axis=0, tiled=True)
    (out,) = call(
        weight_body, "weight", [((64, 40, 128), BF)],
        [full_hidden1, full_tokens, joined, *head_parts], flops=5 * 10**8,
    )
    out = lax.all_to_all(out, SPACE, 0, 0, tiled=True)
    (token_grad,) = call(
        token_body, "token", [((8 * OWN, 128), F32)], [idx, full_grad1, *w1],
        smem=(0,), flops=3 * 10**8,
    )
    out = jnp.sum(out.astype(F32), axis=0)
    local = lax.dynamic_slice(coefs, (0, mine * HEAD), (1, 44))
    halves = jnp.concatenate([out[32:, :44], out[32:, HEAD : HEAD + 44]], axis=0)
    return loss.reshape(()), token_grad, out[16:32], out[:16], (halves * local).T


def solution(mesh):
    inner = Mesh(mesh.devices.reshape(8, 4, 2, 4, 2), ("z", "ya", "yb", "x", "core"))
    return jax.shard_map(
        per_device,
        mesh=inner,
        in_specs=(
            P(SPACE, TENSOR),
            P(None, TENSOR),
            P(None, TENSOR),
            P(TENSOR, None),
            P(TENSOR, SPACE),
            P(None, SPACE),
            P(TENSOR),
            P(),
        ),
        out_specs=(
            P(),
            P(SPACE, TENSOR),
            P(SPACE, TENSOR),
            P(SPACE, TENSOR),
            P(TENSOR, SPACE),
        ),
        check_vma=False,
    )
```

```python
import math

import jax
import jax.numpy as jnp
from jax import lax
from jax.experimental import pallas as pl
from jax.experimental.pallas import tpu as pltpu
from jax.sharding import Mesh
from jax.sharding import PartitionSpec as P

V = 88
PP = 4
LONP = 224
D = 1024
OWN = 112
HEAD = 48
COLS = 8 * HEAD
HALF = 3 * D // 2
PIECE = OWN + 3 * HEAD
BF = jnp.bfloat16
F32 = jnp.float32
SPACE = ("z", "y")
TENSOR = ("x", "core")
OFFS = (0, 3, 1, 2)
PACK = 10**8
BACK = 3 * 10**10
TOKEN = 3 * 10**10


def dot(a, b, da, db):
    return lax.dot_general(a, b, (((da,), (db,)), ((), ())), preferred_element_type=F32)


def lanes(j):
    return pl.ds(pl.multiple_of(j * 128, 128), 128)


def call(body, name, outs, args, smem=(), scratch=(), flops=0, vmem=56, loose=()):
    specs = [
        pl.BlockSpec(
            memory_space=pltpu.SMEM if i in smem else pl.ANY if i in loose else pltpu.VMEM
        )
        for i in range(len(args))
    ]
    return pl.pallas_call(
        body,
        name=name,
        out_shape=tuple(jax.ShapeDtypeStruct(s, t) for s, t in outs),
        in_specs=specs,
        out_specs=tuple(pl.BlockSpec(memory_space=pltpu.VMEM) for _ in outs),
        scratch_shapes=list(scratch),
        compiler_params=pltpu.CompilerParams(vmem_limit_bytes=vmem * 2**20),
        cost_estimate=pl.CostEstimate(flops=flops, bytes_accessed=4 * 2**20, transcendentals=0),
    )(*args)


def prep_body(kinds, tokens, targets, second, head, out, packed):
    real = V * PP // 8
    row = lax.broadcasted_iota(jnp.int32, (HEAD, 128 - OWN), 0)
    kind = jnp.zeros(row.shape, F32)
    for v in range(V // 8):
        kind = jnp.where(row // PP == v, kinds[v].astype(F32), kind)
    blank = jnp.zeros((HEAD - real, 128), F32)
    packed[:D, :] = second[...]
    for i in range(8):
        out[i, :OWN, :] = tokens[OWN * i : OWN * (i + 1), :]
        rest = jnp.concatenate([targets[:, OWN * i : OWN * (i + 1)], kind[:real]], axis=1)
        rest = jnp.concatenate([rest, blank], axis=0)
        for piece in range(3):
            at = OWN + HEAD * piece
            part = rest.astype(BF)
            out[i, at : at + HEAD, :] = part
            rest = rest - part.astype(F32)
        rows = jnp.concatenate([head[:, 128 * i : 128 * (i + 1)].astype(F32), blank], axis=0)
        packed[D + HEAD * i : D + HEAD * (i + 1), :] = rows.astype(BF)


def gelu_parts(z):
    cdf = 0.5 * (1.0 + lax.erf(z * (1.0 / math.sqrt(2.0))))
    return z * cdf, cdf + z * jnp.exp(-0.5 * z * z) * (1.0 / math.sqrt(2.0 * math.pi))


def pairs(refs, rows=slice(0, D)):
    for a in range(2):
        for k in (0, 2):
            both = [refs[a][k, rows, :], refs[a][k + 1, rows, :]]
            yield jnp.concatenate(both, axis=1), 4 * a + k


def layer(idx, value, refs, pre):
    for both, at in pairs(refs):
        z = dot(value, both, 1, 0)
        pre[:, lanes(idx[at])] = z[:, :128]
        pre[:, lanes(idx[at + 1])] = z[:, 128:]
    return gelu_parts(pre[...])


def back_through(idx, grad, refs, rows=slice(0, D)):
    total = None
    for both, at in pairs(refs, rows):
        left = jnp.concatenate([grad[:, lanes(idx[at])], grad[:, lanes(idx[at + 1])]], axis=1)
        term = dot(left, both, 1, 1)
        total = term if total is None else total + term
    return total


def first_body(idx, given, near, far, tokhid, slope1, pre):
    for j in range(8):
        tokhid[:, 128 * j : 128 * (j + 1)] = given[j, :OWN, :]
    hidden, slope = layer(idx, tokhid[:, :D], (near, far), pre)
    tokhid[:, D:] = hidden.astype(BF)
    slope1[...] = slope


def second_body(
    idx, tokhid, given, near, far, land, weights, hidden2, slope2, me, sums, head, pre, goal
):
    for j in range(8):
        parts = [
            given[j, OWN + HEAD * p : OWN + HEAD * (p + 1), :].astype(F32) for p in range(3)
        ]
        goal[HEAD * j : HEAD * (j + 1), :] = parts[0] + (parts[1] + parts[2])
    for a, ref in enumerate((near, far)):
        for s in range(4):
            rows = pl.ds(pl.multiple_of(idx[4 * a + s] * HEAD, HEAD), HEAD)
            for i in range(8):
                piece = ref[s, D + HEAD * i : D + HEAD * (i + 1), :]
                head[rows, 128 * i : 128 * (i + 1)] = piece
    hidden, slope = layer(idx, tokhid[:, D:], (near, far), pre)
    hidden2[...] = hidden.astype(BF)
    slope2[...] = slope
    predicted = dot(hidden2[...], head[...], 1, 1)
    flipped = goal[...].T
    kind = flipped[OWN : OWN + 1, :]
    column = lax.broadcasted_iota(jnp.int32, (8, COLS), 1)
    picks = (column % PP == lax.broadcasted_iota(jnp.int32, (8, COLS), 0)).astype(BF)
    on_land = dot(land[...], picks, 0, 0)[:OWN, :]
    valid = jnp.where(kind == 0.0, 1.0, jnp.where(kind == 1.0, on_land, 1.0 - on_land))
    masked = weights[...] * valid
    error = predicted - flipped[:OWN, :]
    product = masked * error
    me[...] = product
    pair = [jnp.sum(product * error, axis=0, keepdims=True), jnp.sum(masked, axis=0, keepdims=True)]
    sums[...] = jnp.broadcast_to(jnp.concatenate(pair, axis=0)[None], sums.shape)


def spread_body(came, out):
    out[...] = jnp.broadcast_to(jnp.sum(came[...], axis=0, keepdims=True), out.shape)


def pack_body(tokhid, hidden2, came, xh):
    xh[0] = tokhid[:, :HALF]
    xh[1, :, : 2 * D - HALF] = tokhid[:, HALF:]
    xh[1, :, 2 * D - HALF :] = hidden2[...]


def over_cells(v):
    column = lax.broadcasted_iota(jnp.int32, v.shape, 1)
    n = v.shape[1]
    for step in (1, 2):
        ahead = pltpu.roll(v, n - step, 1)
        behind = pltpu.roll(v, step, 1)
        v = v + jnp.where((column // step) % 2 == 0, ahead, behind)
    return v


def backward_body(
    idx, scale, sums, me, slope1, slope2, head, near, far, joined, grad1, loss, g2
):
    total = over_cells(jnp.sum(sums[...], axis=0))
    column = lax.broadcasted_iota(jnp.int32, (1, COLS), 1)
    real = column % HEAD < V * PP // 8
    weight = jnp.where(real, total[1:2, :], 1.0)
    root = jnp.sqrt(total[0:1, :] / weight + 1e-06)
    loss[...] = jnp.sum(jnp.where(real, root, 0.0), axis=1, keepdims=True) / (V * PP)
    coef = jnp.where(real, scale[0] / (V * root * weight), 0.0)
    grad_pred = (coef * me[...]).astype(BF)
    g2[...] = (dot(grad_pred, head[...], 1, 0) * slope2[...]).astype(BF)
    back = back_through(idx, g2, (near, far))
    grad1[...] = (back * slope1[...]).astype(BF)
    for j in range(8):
        joined[j, :, :128] = g2[:, 128 * j : 128 * (j + 1)]
        joined[j, :, 128:256] = grad1[:, 128 * j : 128 * (j + 1)]
        tail = grad_pred[:, HEAD * j : HEAD * (j + 1)].astype(F32)
        tail = jnp.concatenate([tail, jnp.zeros((OWN, 128 - HEAD), F32)], axis=1)
        joined[j, :, 256:] = tail.astype(BF)


def token_body(idx, grad1, near, far, keep, send):
    grad = None
    for both, at in pairs((near, far)):
        left = jnp.concatenate([grad1[:, lanes(idx[at])], grad1[:, lanes(idx[at + 1])]], axis=1)
        term = dot(left, both, 1, 1)
        grad = term if grad is None else grad + term
    mine = idx[8] == 0
    for k in range(4):
        even, odd = grad[:, 256 * k : 256 * k + 128], grad[:, 256 * k + 128 : 256 * (k + 1)]
        keep[k] = jnp.where(mine, even, odd)
        send[k] = jnp.where(mine, odd, even)


def split_body(idx, keep, came, own, up, down, across):
    for ref, off in ((own, 0), (up, 1), (down, 3), (across, 2)):
        k = lax.rem(idx[9] + off, 4)
        ref[0] = keep[k]
        ref[1] = came[k]


def place_body(idx, own, left, right, across, out):
    for s, ref in enumerate((own, left, right, across)):
        for a in range(2):
            rows = pl.ds(pl.multiple_of(idx[4 * a + s] * OWN, OWN), OWN)
            out[rows, :] = ref[a]


def weight_body(idx, near, far, joined, out, order):
    for at in range(8):
        order[OWN * at : OWN * (at + 1), :] = joined[idx[at]]
    half = 4 * OWN
    sums = []
    places = (((1, 0, 512), (0, D, HALF)), ((0, 0, D),), ((1, 512, HALF),))
    for to, cuts in zip((0, 128, 256), (places[0][::-1], places[1], places[2])):
        found = []
        for h, lo, hi in cuts:
            term = dot(order[:half, to : to + 128], near[:, h, :, lo:hi].reshape(half, hi - lo), 0, 0)
            term += dot(order[half:, to : to + 128], far[:, h, :, lo:hi].reshape(half, hi - lo), 0, 0)
            found.append(term.T)
        sums.append(found[0] if len(found) == 1 else jnp.concatenate(found, axis=0))
    part = sums[2].reshape(64, 2, 8, 128)
    high = pltpu.roll(part[:, 1].reshape(512, 128), HEAD, 1).reshape(64, 8, 128)
    wide = [sums[0].reshape(64, 16, 128), sums[1].reshape(64, 16, 128), part[:, 0] + high]
    out[...] = jnp.concatenate(wide, axis=1).astype(BF)


def shift(v, by):
    return lax.ppermute(v, "x", [(i, (i + by) % 4) for i in range(4)])


def flip(v):
    return lax.ppermute(v, "core", [(0, 1), (1, 0)])


def per_device(
    tokens, first_weight, second_weight, head_weight, targets, land_mask, variable_kind, loss_scale
):
    x, core = lax.axis_index("x"), lax.axis_index("core")
    mine = lax.axis_index(TENSOR)
    places = [2 * ((x + off) % 4) + c for c in (core, 1 - core) for off in OFFS]
    idx = jnp.stack([*places, core, x]).astype(jnp.int32)

    given, packed = call(
        prep_body, "prep", [((8, PIECE, 128), BF), ((D + COLS, 128), BF)],
        [variable_kind, tokens, targets, second_weight, head_weight], smem=(0,),
    )
    given = lax.all_to_all(given, TENSOR, 0, 0, tiled=True)
    w1_m1, w1_p1 = shift(first_weight, 1), shift(first_weight, 3)
    w2_m1, w2_p1 = shift(packed, 1), shift(packed, 3)
    w1_m1, w1_p1, w2_m1, w2_p1, given = lax.optimization_barrier((w1_m1, w1_p1, w2_m1, w2_p1, given))
    w1_last, w2_last = shift(w1_m1, 1), shift(w2_p1, 3)
    w1_last, w2_last = lax.optimization_barrier((w1_last, w2_last))
    near1 = jnp.stack([first_weight, w1_m1, w1_p1, w1_last])
    near2 = jnp.stack([packed, w2_m1, w2_p1, w2_last])
    far1, far2 = flip(near1), flip(near2)

    land = lax.dynamic_slice(land_mask, (0, mine * OWN), (PP, OWN))
    land = jnp.pad(land.astype(BF), ((0, 8 - PP), (0, 128 - OWN)))
    space = lax.axis_index(SPACE)
    patch_row = (space * 8 * OWN + mine * OWN) // LONP
    nlat = 2 * (64 * 8 * OWN // LONP)
    col = jnp.arange(COLS, dtype=jnp.int32)
    lat_row = 2 * patch_row + (col % PP) // 2
    weights = jnp.cos(math.pi / 2.0 * (lat_row.astype(F32) + 0.5) / nlat)
    weights = jnp.where(col % HEAD < 44, weights, 0.0)[None, :]

    tokhid, slope1 = call(
        first_body, "first", [((OWN, 2 * D), BF), ((OWN, D), F32)], [idx, given, near1, far1],
        smem=(0,), scratch=[pltpu.VMEM((OWN, D), F32)], flops=3 * 10**8,
    )
    hidden2, slope2, me, sums, head = call(
        second_body, "second",
        [((OWN, D), BF), ((OWN, D), F32), ((OWN, COLS), F32), ((8, 2, COLS), F32), ((COLS, D), BF)],
        [idx, tokhid, given, near2, far2, land, weights], smem=(0,),
        scratch=[pltpu.VMEM((OWN, D), F32), pltpu.VMEM((COLS, 128), F32)], flops=5 * 10**8,
    )

    sums = lax.all_to_all(sums, TENSOR, 0, 0, tiled=True)
    (spread,) = call(spread_body, "spread", [((64, 2, COLS), F32)], [sums])
    (xh,) = call(
        pack_body, "pack", [((2, OWN, HALF), BF)], [tokhid, hidden2, sums], loose=(2,),
        flops=PACK,
    )
    sums = lax.all_to_all(spread, SPACE, 0, 0, tiled=True)

    xh_m1, xh_p1 = shift(xh, 1), shift(xh, 3)
    xh_last = jnp.stack([shift(xh_m1[0], 1), shift(xh_p1[1], 3)])
    xhn = jnp.stack([xh, xh_m1, xh_p1, xh_last])
    xhf = flip(xhn)

    joined, grad1, loss = call(
        backward_body, "backward",
        [((8, OWN, 384), BF), ((OWN, D), BF), ((1, 1), F32)],
        [idx, loss_scale.reshape(1), sums, me, slope1, slope2, head, near2, far2],
        smem=(0, 1), scratch=[pltpu.VMEM((OWN, D), BF)], flops=BACK,
    )
    joined = lax.all_to_all(joined, TENSOR, 0, 0, tiled=True)
    (out,) = call(
        weight_body, "weight", [((64, 40, 128), BF)], [idx, xhn, xhf, joined], smem=(0,),
        scratch=[pltpu.VMEM((8 * OWN, 384), BF)], flops=8 * 10**8,
    )
    keep, send = call(
        token_body, "token", [((4, OWN, 128), F32)] * 2, [idx, grad1, near1, far1], smem=(0,),
        flops=TOKEN,
    )
    came, keep, out = lax.optimization_barrier((flip(send), keep, out))
    out = lax.all_to_all(out, SPACE, 0, 0, tiled=True)
    own, up, down, across = call(
        split_body, "split", [((2, OWN, 128), F32)] * 4, [idx, keep, came], smem=(0,)
    )
    (token_grad,) = call(
        place_body, "place", [((8 * OWN, 128), F32)],
        [idx, own, shift(up, 1), shift(down, 3), shift(across, 2)], smem=(0,),
    )
    out = jnp.sum(out.astype(F32), axis=0)
    halves = jnp.concatenate([out[32:, :44], out[32:, HEAD : HEAD + 44]], axis=0)
    return loss.reshape(()), token_grad, out[16:32], out[:16], halves.T


def solution(mesh):
    inner = Mesh(mesh.devices.reshape(8, 8, 4, 2), ("z", "y", "x", "core"))
    return jax.shard_map(
        per_device,
        mesh=inner,
        in_specs=(
            P(SPACE, TENSOR),
            P(None, TENSOR),
            P(None, TENSOR),
            P(TENSOR, None),
            P(TENSOR, SPACE),
            P(None, SPACE),
            P(TENSOR),
            P(),
        ),
        out_specs=(
            P(),
            P(SPACE, TENSOR),
            P(SPACE, TENSOR),
            P(SPACE, TENSOR),
            P(TENSOR, SPACE),
        ),
        check_vma=False,
    )
```

```python
import math

import jax
import jax.numpy as jnp
from jax import lax
from jax.experimental import pallas as pl
from jax.experimental.pallas import tpu as pltpu
from jax.sharding import Mesh
from jax.sharding import PartitionSpec as P

V = 88
PP = 4
LONP = 224
D = 1024
OWN = 112
HEAD = 48
COLS = 8 * HEAD
HALF = 3 * D // 2
PIECE = OWN + 3 * HEAD
BF = jnp.bfloat16
F32 = jnp.float32
SPACE = ("z", "y")
TENSOR = ("x", "core")
OFFS = (0, 3, 1, 2)
PACK = 10**8
FIRST = 2 * 10**10
BACK = 3 * 10**10
TOKEN = 3 * 10**10


def dot(a, b, da, db):
    return lax.dot_general(a, b, (((da,), (db,)), ((), ())), preferred_element_type=F32)


def lanes(j):
    return pl.ds(pl.multiple_of(j * 128, 128), 128)


def call(body, name, outs, args, smem=(), scratch=(), flops=0, vmem=56, loose=()):
    specs = [
        pl.BlockSpec(
            memory_space=pltpu.SMEM if i in smem else pl.ANY if i in loose else pltpu.VMEM
        )
        for i in range(len(args))
    ]
    return pl.pallas_call(
        body,
        name=name,
        out_shape=tuple(jax.ShapeDtypeStruct(s, t) for s, t in outs),
        in_specs=specs,
        out_specs=tuple(pl.BlockSpec(memory_space=pltpu.VMEM) for _ in outs),
        scratch_shapes=list(scratch),
        compiler_params=pltpu.CompilerParams(vmem_limit_bytes=vmem * 2**20),
        cost_estimate=pl.CostEstimate(flops=flops, bytes_accessed=4 * 2**20, transcendentals=0),
    )(*args)


def prep_body(kinds, tokens, targets, second, head, out, packed):
    real = V * PP // 8
    row = lax.broadcasted_iota(jnp.int32, (HEAD, 128 - OWN), 0)
    kind = jnp.zeros(row.shape, F32)
    for v in range(V // 8):
        kind = jnp.where(row // PP == v, kinds[v].astype(F32), kind)
    blank = jnp.zeros((HEAD - real, 128), F32)
    packed[:D, :] = second[...]
    for i in range(8):
        out[i, :OWN, :] = tokens[OWN * i : OWN * (i + 1), :]
        rest = jnp.concatenate([targets[:, OWN * i : OWN * (i + 1)], kind[:real]], axis=1)
        rest = jnp.concatenate([rest, blank], axis=0)
        for piece in range(3):
            at = OWN + HEAD * piece
            part = rest.astype(BF)
            out[i, at : at + HEAD, :] = part
            rest = rest - part.astype(F32)
        rows = jnp.concatenate([head[:, 128 * i : 128 * (i + 1)].astype(F32), blank], axis=0)
        packed[D + HEAD * i : D + HEAD * (i + 1), :] = rows.astype(BF)


def gelu_parts(z):
    cdf = 0.5 * (1.0 + lax.erf(z * (1.0 / math.sqrt(2.0))))
    return z * cdf, cdf + z * jnp.exp(-0.5 * z * z) * (1.0 / math.sqrt(2.0 * math.pi))


def pairs(refs, rows=slice(0, D)):
    for a in range(2):
        for k in (0, 2):
            both = [refs[a][k, rows, :], refs[a][k + 1, rows, :]]
            yield jnp.concatenate(both, axis=1), 4 * a + k


def layer(idx, value, refs, pre):
    for both, at in pairs(refs):
        z = dot(value, both, 1, 0)
        pre[:, lanes(idx[at])] = z[:, :128]
        pre[:, lanes(idx[at + 1])] = z[:, 128:]
    return gelu_parts(pre[...])


def back_through(idx, grad, refs, rows=slice(0, D)):
    total = None
    for both, at in pairs(refs, rows):
        left = jnp.concatenate([grad[:, lanes(idx[at])], grad[:, lanes(idx[at + 1])]], axis=1)
        term = dot(left, both, 1, 1)
        total = term if total is None else total + term
    return total


def first_body(idx, given, near, far, tokhid, slope1, pre):
    for j in range(8):
        tokhid[:, 128 * j : 128 * (j + 1)] = given[j, :OWN, :]
    hidden, slope = layer(idx, tokhid[:, :D], (near, far), pre)
    tokhid[:, D:] = hidden.astype(BF)
    slope1[...] = slope


def second_body(
    idx, tokhid, given, near, far, land, weights, hidden2, slope2, me, sums, head, pre, goal
):
    for j in range(8):
        parts = [
            given[j, OWN + HEAD * p : OWN + HEAD * (p + 1), :].astype(F32) for p in range(3)
        ]
        goal[HEAD * j : HEAD * (j + 1), :] = parts[0] + (parts[1] + parts[2])
    for a, ref in enumerate((near, far)):
        for s in range(4):
            rows = pl.ds(pl.multiple_of(idx[4 * a + s] * HEAD, HEAD), HEAD)
            for i in range(8):
                piece = ref[s, D + HEAD * i : D + HEAD * (i + 1), :]
                head[rows, 128 * i : 128 * (i + 1)] = piece
    hidden, slope = layer(idx, tokhid[:, D:], (near, far), pre)
    hidden2[...] = hidden.astype(BF)
    slope2[...] = slope
    predicted = dot(hidden2[...], head[...], 1, 1)
    flipped = goal[...].T
    kind = flipped[OWN : OWN + 1, :]
    column = lax.broadcasted_iota(jnp.int32, (8, COLS), 1)
    picks = (column % PP == lax.broadcasted_iota(jnp.int32, (8, COLS), 0)).astype(BF)
    on_land = dot(land[...], picks, 0, 0)[:OWN, :]
    valid = jnp.where(kind == 0.0, 1.0, jnp.where(kind == 1.0, on_land, 1.0 - on_land))
    masked = weights[...] * valid
    error = predicted - flipped[:OWN, :]
    product = masked * error
    me[...] = product
    pair = [jnp.sum(product * error, axis=0, keepdims=True), jnp.sum(masked, axis=0, keepdims=True)]
    sums[...] = jnp.broadcast_to(jnp.concatenate(pair, axis=0)[None], sums.shape)


def spread_body(came, out):
    out[...] = jnp.broadcast_to(jnp.sum(came[...], axis=0, keepdims=True), out.shape)


def pack_body(tokhid, hidden2, came, xh):
    xh[0] = tokhid[:, :HALF]
    xh[1, :, : 2 * D - HALF] = tokhid[:, HALF:]
    xh[1, :, 2 * D - HALF :] = hidden2[...]


def over_cells(v):
    column = lax.broadcasted_iota(jnp.int32, v.shape, 1)
    n = v.shape[1]
    for step in (1, 2):
        ahead = pltpu.roll(v, n - step, 1)
        behind = pltpu.roll(v, step, 1)
        v = v + jnp.where((column // step) % 2 == 0, ahead, behind)
    return v


def backward_body(
    idx, scale, sums, me, slope1, slope2, head, near, far, joined, grad1, loss, g2
):
    total = over_cells(jnp.sum(sums[...], axis=0))
    column = lax.broadcasted_iota(jnp.int32, (1, COLS), 1)
    real = column % HEAD < V * PP // 8
    weight = jnp.where(real, total[1:2, :], 1.0)
    root = jnp.sqrt(total[0:1, :] / weight + 1e-06)
    loss[...] = jnp.sum(jnp.where(real, root, 0.0), axis=1, keepdims=True) / (V * PP)
    coef = jnp.where(real, scale[0] / (V * root * weight), 0.0)
    grad_pred = (coef * me[...]).astype(BF)
    g2[...] = (dot(grad_pred, head[...], 1, 0) * slope2[...]).astype(BF)
    back = back_through(idx, g2, (near, far))
    grad1[...] = (back * slope1[...]).astype(BF)
    for j in range(8):
        joined[j, :, :128] = g2[:, 128 * j : 128 * (j + 1)]
        joined[j, :, 128:256] = grad1[:, 128 * j : 128 * (j + 1)]
        tail = grad_pred[:, HEAD * j : HEAD * (j + 1)].astype(F32)
        tail = jnp.concatenate([tail, jnp.zeros((OWN, 128 - HEAD), F32)], axis=1)
        joined[j, :, 256:] = tail.astype(BF)


def token_body(idx, grad1, near, far, keep, send):
    grad = None
    for both, at in pairs((near, far)):
        left = jnp.concatenate([grad1[:, lanes(idx[at])], grad1[:, lanes(idx[at + 1])]], axis=1)
        term = dot(left, both, 1, 1)
        grad = term if grad is None else grad + term
    mine = idx[8] == 0
    for k in range(4):
        even, odd = grad[:, 256 * k : 256 * k + 128], grad[:, 256 * k + 128 : 256 * (k + 1)]
        keep[k] = jnp.where(mine, even, odd)
        send[k] = jnp.where(mine, odd, even)


def split_body(idx, keep, came, own, up, down, across):
    for ref, off in ((own, 0), (up, 1), (down, 3), (across, 2)):
        k = lax.rem(idx[9] + off, 4)
        ref[0] = keep[k]
        ref[1] = came[k]


def place_body(idx, own, left, right, across, out):
    for s, ref in enumerate((own, left, right, across)):
        for a in range(2):
            rows = pl.ds(pl.multiple_of(idx[4 * a + s] * OWN, OWN), OWN)
            out[rows, :] = ref[a]


def weight_body(idx, near, far, joined, out, order):
    for at in range(8):
        order[OWN * at : OWN * (at + 1), :] = joined[idx[at]]
    half = 4 * OWN
    sums = []
    places = (((1, 0, 512), (0, D, HALF)), ((0, 0, D),), ((1, 512, HALF),))
    for to, cuts in zip((0, 128, 256), (places[0][::-1], places[1], places[2])):
        found = []
        for h, lo, hi in cuts:
            term = dot(order[:half, to : to + 128], near[:, h, :, lo:hi].reshape(half, hi - lo), 0, 0)
            term += dot(order[half:, to : to + 128], far[:, h, :, lo:hi].reshape(half, hi - lo), 0, 0)
            found.append(term.T)
        sums.append(found[0] if len(found) == 1 else jnp.concatenate(found, axis=0))
    part = sums[2].reshape(64, 2, 8, 128)
    high = pltpu.roll(part[:, 1].reshape(512, 128), HEAD, 1).reshape(64, 8, 128)
    wide = [sums[0].reshape(64, 16, 128), sums[1].reshape(64, 16, 128), part[:, 0] + high]
    out[...] = jnp.concatenate(wide, axis=1).astype(BF)


def shift(v, by):
    return lax.ppermute(v, "x", [(i, (i + by) % 4) for i in range(4)])


def flip(v):
    return lax.ppermute(v, "core", [(0, 1), (1, 0)])


def per_device(
    tokens, first_weight, second_weight, head_weight, targets, land_mask, variable_kind, loss_scale
):
    x, core = lax.axis_index("x"), lax.axis_index("core")
    mine = lax.axis_index(TENSOR)
    places = [2 * ((x + off) % 4) + c for c in (core, 1 - core) for off in OFFS]
    idx = jnp.stack([*places, core, x]).astype(jnp.int32)

    given, packed = call(
        prep_body, "prep", [((8, PIECE, 128), BF), ((D + COLS, 128), BF)],
        [variable_kind, tokens, targets, second_weight, head_weight], smem=(0,),
    )
    given = lax.all_to_all(given, TENSOR, 0, 0, tiled=True)
    w1_m1, w1_p1 = shift(first_weight, 1), shift(first_weight, 3)
    w2_m1, w2_p1 = shift(packed, 1), shift(packed, 3)
    w1_m1, w1_p1, w2_m1, w2_p1, given = lax.optimization_barrier((w1_m1, w1_p1, w2_m1, w2_p1, given))
    w1_last, w2_last = shift(w1_m1, 1), shift(w2_p1, 3)
    w1_last, w2_last = lax.optimization_barrier((w1_last, w2_last))
    near1 = jnp.stack([first_weight, w1_m1, w1_p1, w1_last])
    near2 = jnp.stack([packed, w2_m1, w2_p1, w2_last])
    far1, far2 = flip(near1), flip(near2)

    land = lax.dynamic_slice(land_mask, (0, mine * OWN), (PP, OWN))
    land = jnp.pad(land.astype(BF), ((0, 8 - PP), (0, 128 - OWN)))
    space = lax.axis_index(SPACE)
    patch_row = (space * 8 * OWN + mine * OWN) // LONP
    nlat = 2 * (64 * 8 * OWN // LONP)
    col = jnp.arange(COLS, dtype=jnp.int32)
    lat_row = 2 * patch_row + (col % PP) // 2
    weights = jnp.cos(math.pi / 2.0 * (lat_row.astype(F32) + 0.5) / nlat)
    weights = jnp.where(col % HEAD < 44, weights, 0.0)[None, :]

    tokhid, slope1 = call(
        first_body, "first", [((OWN, 2 * D), BF), ((OWN, D), F32)], [idx, given, near1, far1],
        smem=(0,), scratch=[pltpu.VMEM((OWN, D), F32)], flops=FIRST,
    )
    hidden2, slope2, me, sums, head = call(
        second_body, "second",
        [((OWN, D), BF), ((OWN, D), F32), ((OWN, COLS), F32), ((8, 2, COLS), F32), ((COLS, D), BF)],
        [idx, tokhid, given, near2, far2, land, weights], smem=(0,),
        scratch=[pltpu.VMEM((OWN, D), F32), pltpu.VMEM((COLS, 128), F32)], flops=5 * 10**8,
    )

    sums = lax.all_to_all(sums, TENSOR, 0, 0, tiled=True)
    (spread,) = call(spread_body, "spread", [((64, 2, COLS), F32)], [sums])
    (xh,) = call(
        pack_body, "pack", [((2, OWN, HALF), BF)], [tokhid, hidden2, spread], loose=(2,),
        flops=PACK,
    )
    sums = lax.all_to_all(spread, SPACE, 0, 0, tiled=True)

    xhn = jnp.stack([xh, shift(xh, 1), shift(xh, 3), shift(xh, 2)])
    xhf = flip(xhn)

    joined, grad1, loss = call(
        backward_body, "backward",
        [((8, OWN, 384), BF), ((OWN, D), BF), ((1, 1), F32)],
        [idx, loss_scale.reshape(1), sums, me, slope1, slope2, head, near2, far2],
        smem=(0, 1), scratch=[pltpu.VMEM((OWN, D), BF)], flops=BACK,
    )
    joined = lax.all_to_all(joined, TENSOR, 0, 0, tiled=True)
    (out,) = call(
        weight_body, "weight", [((64, 40, 128), BF)], [idx, xhn, xhf, joined], smem=(0,),
        scratch=[pltpu.VMEM((8 * OWN, 384), BF)], flops=8 * 10**8,
    )
    keep, send = call(
        token_body, "token", [((4, OWN, 128), F32)] * 2, [idx, grad1, near1, far1], smem=(0,),
        flops=TOKEN,
    )
    came, keep, out = lax.optimization_barrier((flip(send), keep, out))
    out = lax.all_to_all(out, SPACE, 0, 0, tiled=True)
    own, up, down, across = call(
        split_body, "split", [((2, OWN, 128), F32)] * 4, [idx, keep, came], smem=(0,)
    )
    (token_grad,) = call(
        place_body, "place", [((8 * OWN, 128), F32)],
        [idx, own, shift(up, 1), shift(down, 3), shift(across, 2)], smem=(0,),
    )
    out = jnp.sum(out.astype(F32), axis=0)
    halves = jnp.concatenate([out[32:, :44], out[32:, HEAD : HEAD + 44]], axis=0)
    return loss.reshape(()), token_grad, out[16:32], out[:16], halves.T


def solution(mesh):
    inner = Mesh(mesh.devices.reshape(8, 8, 4, 2), ("z", "y", "x", "core"))
    return jax.shard_map(
        per_device,
        mesh=inner,
        in_specs=(
            P(SPACE, TENSOR),
            P(None, TENSOR),
            P(None, TENSOR),
            P(TENSOR, None),
            P(TENSOR, SPACE),
            P(None, SPACE),
            P(TENSOR),
            P(),
        ),
        out_specs=(
            P(),
            P(SPACE, TENSOR),
            P(SPACE, TENSOR),
            P(SPACE, TENSOR),
            P(TENSOR, SPACE),
        ),
        check_vma=False,
    )
```

```python
import math

import jax
import jax.numpy as jnp
from jax import lax
from jax.experimental import pallas as pl
from jax.experimental.pallas import tpu as pltpu
from jax.sharding import Mesh
from jax.sharding import PartitionSpec as P

V = 88
PP = 4
LONP = 224
D = 1024
OWN = 112
HEAD = 48
COLS = 8 * HEAD
HALF = 3 * D // 2
PIECE = OWN + 3 * HEAD
BF = jnp.bfloat16
F32 = jnp.float32
SPACE = ("z", "y")
TENSOR = ("x", "core")
OFFS = (0, 3, 1, 2)
FIRST = 2 * 10**10
BACK = 3 * 10**10
TOKEN = 3 * 10**10


def dot(a, b, da, db):
    return lax.dot_general(a, b, (((da,), (db,)), ((), ())), preferred_element_type=F32)


def lanes(j):
    return pl.ds(pl.multiple_of(j * 128, 128), 128)


def call(body, name, outs, args, smem=(), scratch=(), flops=0, vmem=56, loose=()):
    specs = [
        pl.BlockSpec(
            memory_space=pltpu.SMEM if i in smem else pl.ANY if i in loose else pltpu.VMEM
        )
        for i in range(len(args))
    ]
    return pl.pallas_call(
        body,
        name=name,
        out_shape=tuple(jax.ShapeDtypeStruct(s, t) for s, t in outs),
        in_specs=specs,
        out_specs=tuple(pl.BlockSpec(memory_space=pltpu.VMEM) for _ in outs),
        scratch_shapes=list(scratch),
        compiler_params=pltpu.CompilerParams(vmem_limit_bytes=vmem * 2**20),
        cost_estimate=pl.CostEstimate(flops=flops, bytes_accessed=4 * 2**20, transcendentals=0),
    )(*args)


def prep_body(kinds, tokens, targets, second, head, out, packed):
    real = V * PP // 8
    row = lax.broadcasted_iota(jnp.int32, (HEAD, 128 - OWN), 0)
    kind = jnp.zeros(row.shape, F32)
    for v in range(V // 8):
        kind = jnp.where(row // PP == v, kinds[v].astype(F32), kind)
    blank = jnp.zeros((HEAD - real, 128), F32)
    packed[:D, :] = second[...]
    for i in range(8):
        out[i, :OWN, :] = tokens[OWN * i : OWN * (i + 1), :]
        rest = jnp.concatenate([targets[:, OWN * i : OWN * (i + 1)], kind[:real]], axis=1)
        rest = jnp.concatenate([rest, blank], axis=0)
        for piece in range(3):
            at = OWN + HEAD * piece
            part = rest.astype(BF)
            out[i, at : at + HEAD, :] = part
            rest = rest - part.astype(F32)
        rows = jnp.concatenate([head[:, 128 * i : 128 * (i + 1)].astype(F32), blank], axis=0)
        packed[D + HEAD * i : D + HEAD * (i + 1), :] = rows.astype(BF)


def gelu_parts(z):
    cdf = 0.5 * (1.0 + lax.erf(z * (1.0 / math.sqrt(2.0))))
    return z * cdf, cdf + z * jnp.exp(-0.5 * z * z) * (1.0 / math.sqrt(2.0 * math.pi))


def pairs(refs, rows=slice(0, D)):
    for a in range(2):
        for k in (0, 2):
            both = [refs[a][k, rows, :], refs[a][k + 1, rows, :]]
            yield jnp.concatenate(both, axis=1), 4 * a + k


def layer(idx, value, refs, pre):
    for both, at in pairs(refs):
        z = dot(value, both, 1, 0)
        pre[:, lanes(idx[at])] = z[:, :128]
        pre[:, lanes(idx[at + 1])] = z[:, 128:]
    return gelu_parts(pre[...])


def back_through(idx, grad, refs, rows=slice(0, D)):
    total = None
    for both, at in pairs(refs, rows):
        left = jnp.concatenate([grad[:, lanes(idx[at])], grad[:, lanes(idx[at + 1])]], axis=1)
        term = dot(left, both, 1, 1)
        total = term if total is None else total + term
    return total


def first_body(idx, given, near, far, tokhid, slope1, pre):
    for j in range(8):
        tokhid[:, 128 * j : 128 * (j + 1)] = given[j, :OWN, :]
    hidden, slope = layer(idx, tokhid[:, :D], (near, far), pre)
    tokhid[:, D:] = hidden.astype(BF)
    slope1[...] = slope


def second_body(
    idx, tokhid, given, near, far, land, weights, xh, slope2, me, sums, head, pre, goal
):
    for j in range(8):
        parts = [
            given[j, OWN + HEAD * p : OWN + HEAD * (p + 1), :].astype(F32) for p in range(3)
        ]
        goal[HEAD * j : HEAD * (j + 1), :] = parts[0] + (parts[1] + parts[2])
    for a, ref in enumerate((near, far)):
        for s in range(4):
            rows = pl.ds(pl.multiple_of(idx[4 * a + s] * HEAD, HEAD), HEAD)
            for i in range(8):
                piece = ref[s, D + HEAD * i : D + HEAD * (i + 1), :]
                head[rows, 128 * i : 128 * (i + 1)] = piece
    hidden, slope = layer(idx, tokhid[:, D:], (near, far), pre)
    hidden2 = hidden.astype(BF)
    xh[0] = tokhid[:, :HALF]
    xh[1, :, : 2 * D - HALF] = tokhid[:, HALF:]
    xh[1, :, 2 * D - HALF :] = hidden2
    slope2[...] = slope
    predicted = dot(hidden2, head[...], 1, 1)
    flipped = goal[...].T
    kind = flipped[OWN : OWN + 1, :]
    column = lax.broadcasted_iota(jnp.int32, (8, COLS), 1)
    picks = (column % PP == lax.broadcasted_iota(jnp.int32, (8, COLS), 0)).astype(BF)
    on_land = dot(land[...], picks, 0, 0)[:OWN, :]
    valid = jnp.where(kind == 0.0, 1.0, jnp.where(kind == 1.0, on_land, 1.0 - on_land))
    masked = weights[...] * valid
    error = predicted - flipped[:OWN, :]
    product = masked * error
    me[...] = product
    pair = [jnp.sum(product * error, axis=0, keepdims=True), jnp.sum(masked, axis=0, keepdims=True)]
    sums[...] = jnp.broadcast_to(jnp.concatenate(pair, axis=0)[None], sums.shape)


def over_cells(v):
    column = lax.broadcasted_iota(jnp.int32, v.shape, 1)
    n = v.shape[1]
    for step in (1, 2):
        ahead = pltpu.roll(v, n - step, 1)
        behind = pltpu.roll(v, step, 1)
        v = v + jnp.where((column // step) % 2 == 0, ahead, behind)
    return v


def backward_body(
    idx, scale, sums, me, slope1, slope2, head, near, far, joined, grad1, loss, g2
):
    total = over_cells(jnp.sum(sums[...], axis=0))
    column = lax.broadcasted_iota(jnp.int32, (1, COLS), 1)
    real = column % HEAD < V * PP // 8
    weight = jnp.where(real, total[1:2, :], 1.0)
    root = jnp.sqrt(total[0:1, :] / weight + 1e-06)
    loss[...] = jnp.sum(jnp.where(real, root, 0.0), axis=1, keepdims=True) / (V * PP)
    coef = jnp.where(real, scale[0] / (V * root * weight), 0.0)
    grad_pred = (coef * me[...]).astype(BF)
    g2[...] = (dot(grad_pred, head[...], 1, 0) * slope2[...]).astype(BF)
    back = back_through(idx, g2, (near, far))
    grad1[...] = (back * slope1[...]).astype(BF)
    for j in range(8):
        joined[j, :, :128] = g2[:, 128 * j : 128 * (j + 1)]
        joined[j, :, 128:256] = grad1[:, 128 * j : 128 * (j + 1)]
        tail = grad_pred[:, HEAD * j : HEAD * (j + 1)].astype(F32)
        tail = jnp.concatenate([tail, jnp.zeros((OWN, 128 - HEAD), F32)], axis=1)
        joined[j, :, 256:] = tail.astype(BF)


def token_body(idx, grad1, near, far, keep, send):
    grad = None
    for both, at in pairs((near, far)):
        left = jnp.concatenate([grad1[:, lanes(idx[at])], grad1[:, lanes(idx[at + 1])]], axis=1)
        term = dot(left, both, 1, 1)
        grad = term if grad is None else grad + term
    mine = idx[8] == 0
    for k in range(4):
        even, odd = grad[:, 256 * k : 256 * k + 128], grad[:, 256 * k + 128 : 256 * (k + 1)]
        keep[k] = jnp.where(mine, even, odd)
        send[k] = jnp.where(mine, odd, even)


def split_body(idx, keep, came, own, up, down, across):
    for ref, off in ((own, 0), (up, 1), (down, 3), (across, 2)):
        k = lax.rem(idx[9] + off, 4)
        ref[0] = keep[k]
        ref[1] = came[k]


def place_body(idx, own, left, right, across, out):
    for s, ref in enumerate((own, left, right, across)):
        for a in range(2):
            rows = pl.ds(pl.multiple_of(idx[4 * a + s] * OWN, OWN), OWN)
            out[rows, :] = ref[a]


def weight_body(idx, near, far, joined, out, order):
    for at in range(8):
        order[OWN * at : OWN * (at + 1), :] = joined[idx[at]]
    half = 4 * OWN
    sums = []
    places = (((1, 0, 512), (0, D, HALF)), ((0, 0, D),), ((1, 512, HALF),))
    for to, cuts in zip((0, 128, 256), (places[0][::-1], places[1], places[2])):
        found = []
        for h, lo, hi in cuts:
            term = dot(order[:half, to : to + 128], near[:, h, :, lo:hi].reshape(half, hi - lo), 0, 0)
            term += dot(order[half:, to : to + 128], far[:, h, :, lo:hi].reshape(half, hi - lo), 0, 0)
            found.append(term.T)
        sums.append(found[0] if len(found) == 1 else jnp.concatenate(found, axis=0))
    part = sums[2].reshape(64, 2, 8, 128)
    high = pltpu.roll(part[:, 1].reshape(512, 128), HEAD, 1).reshape(64, 8, 128)
    wide = [sums[0].reshape(64, 16, 128), sums[1].reshape(64, 16, 128), part[:, 0] + high]
    out[...] = jnp.concatenate(wide, axis=1).astype(BF)


def shift(v, by):
    return lax.ppermute(v, "x", [(i, (i + by) % 4) for i in range(4)])


def flip(v):
    return lax.ppermute(v, "core", [(0, 1), (1, 0)])


def per_device(
    tokens, first_weight, second_weight, head_weight, targets, land_mask, variable_kind, loss_scale
):
    x, core = lax.axis_index("x"), lax.axis_index("core")
    mine = lax.axis_index(TENSOR)
    places = [2 * ((x + off) % 4) + c for c in (core, 1 - core) for off in OFFS]
    idx = jnp.stack([*places, core, x]).astype(jnp.int32)

    land = lax.dynamic_slice(land_mask, (0, mine * OWN), (PP, OWN))
    land = jnp.pad(land.astype(BF), ((0, 8 - PP), (0, 128 - OWN)))
    space = lax.axis_index(SPACE)
    patch_row = (space * 8 * OWN + mine * OWN) // LONP
    nlat = 2 * (64 * 8 * OWN // LONP)
    col = jnp.arange(COLS, dtype=jnp.int32)
    lat_row = 2 * patch_row + (col % PP) // 2
    weights = jnp.cos(math.pi / 2.0 * (lat_row.astype(F32) + 0.5) / nlat)
    weights = jnp.where(col % HEAD < 44, weights, 0.0)[None, :]

    given, packed = call(
        prep_body, "prep", [((8, PIECE, 128), BF), ((D + COLS, 128), BF)],
        [variable_kind, tokens, targets, second_weight, head_weight], smem=(0,),
    )
    given = lax.all_to_all(given, TENSOR, 0, 0, tiled=True)
    w1_m1, w1_p1 = shift(first_weight, 1), shift(first_weight, 3)
    w2_m1, w2_p1 = shift(packed, 1), shift(packed, 3)
    w1_m1, w1_p1, w2_m1, w2_p1, given, idx, land, weights = lax.optimization_barrier(
        (w1_m1, w1_p1, w2_m1, w2_p1, given, idx, land, weights)
    )
    w1_last, w2_last = shift(w1_m1, 1), shift(w2_p1, 3)
    w1_last, w2_last = lax.optimization_barrier((w1_last, w2_last))
    near1 = jnp.stack([first_weight, w1_m1, w1_p1, w1_last])
    near2 = jnp.stack([packed, w2_m1, w2_p1, w2_last])
    far1, far2 = flip(near1), flip(near2)

    tokhid, slope1 = call(
        first_body, "first", [((OWN, 2 * D), BF), ((OWN, D), F32)], [idx, given, near1, far1],
        smem=(0,), scratch=[pltpu.VMEM((OWN, D), F32)], flops=FIRST,
    )
    xh, slope2, me, sums, head = call(
        second_body, "second",
        [((2, OWN, HALF), BF), ((OWN, D), F32), ((OWN, COLS), F32), ((8, 2, COLS), F32),
         ((COLS, D), BF)],
        [idx, tokhid, given, near2, far2, land, weights], smem=(0,),
        scratch=[pltpu.VMEM((OWN, D), F32), pltpu.VMEM((COLS, 128), F32)], flops=5 * 10**8,
    )

    sums = lax.all_to_all(sums, TENSOR, 0, 0, tiled=True)
    sums, xh = lax.optimization_barrier((sums, xh))
    spread = jnp.broadcast_to(jnp.sum(sums, axis=0), (64, 2, COLS))
    sums = lax.all_to_all(spread, SPACE, 0, 0, tiled=True)

    xh_m1, xh_p1 = shift(xh, 1), shift(xh, 3)
    xh_last = jnp.stack([shift(xh_m1[0], 1), shift(xh_p1[1], 3)])
    xhn = jnp.stack([xh, xh_m1, xh_p1, xh_last])
    xhf = flip(xhn)

    joined, grad1, loss = call(
        backward_body, "backward",
        [((8, OWN, 384), BF), ((OWN, D), BF), ((1, 1), F32)],
        [idx, loss_scale.reshape(1), sums, me, slope1, slope2, head, near2, far2],
        smem=(0, 1), scratch=[pltpu.VMEM((OWN, D), BF)], flops=BACK,
    )
    joined = lax.all_to_all(joined, TENSOR, 0, 0, tiled=True)
    (out,) = call(
        weight_body, "weight", [((64, 40, 128), BF)], [idx, xhn, xhf, joined], smem=(0,),
        scratch=[pltpu.VMEM((8 * OWN, 384), BF)], flops=8 * 10**8,
    )
    keep, send = call(
        token_body, "token", [((4, OWN, 128), F32)] * 2, [idx, grad1, near1, far1], smem=(0,),
        flops=TOKEN,
    )
    came, keep, out = lax.optimization_barrier((flip(send), keep, out))
    out = lax.all_to_all(out, SPACE, 0, 0, tiled=True)
    own, up, down, across = call(
        split_body, "split", [((2, OWN, 128), F32)] * 4, [idx, keep, came], smem=(0,)
    )
    (token_grad,) = call(
        place_body, "place", [((8 * OWN, 128), F32)],
        [idx, own, shift(up, 1), shift(down, 3), shift(across, 2)], smem=(0,),
    )
    out = jnp.sum(out.astype(F32), axis=0)
    halves = jnp.concatenate([out[32:, :44], out[32:, HEAD : HEAD + 44]], axis=0)
    return loss.reshape(()), token_grad, out[16:32], out[:16], halves.T


def solution(mesh):
    inner = Mesh(mesh.devices.reshape(8, 8, 4, 2), ("z", "y", "x", "core"))
    return jax.shard_map(
        per_device,
        mesh=inner,
        in_specs=(
            P(SPACE, TENSOR),
            P(None, TENSOR),
            P(None, TENSOR),
            P(TENSOR, None),
            P(TENSOR, SPACE),
            P(None, SPACE),
            P(TENSOR),
            P(),
        ),
        out_specs=(
            P(),
            P(SPACE, TENSOR),
            P(SPACE, TENSOR),
            P(SPACE, TENSOR),
            P(TENSOR, SPACE),
        ),
        check_vma=False,
    )
```

```python
import math

import jax
import jax.numpy as jnp
from jax import lax
from jax.experimental import pallas as pl
from jax.experimental.pallas import tpu as pltpu
from jax.sharding import Mesh
from jax.sharding import PartitionSpec as P

V = 88
PP = 4
LONP = 224
D = 1024
OWN = 112
HEAD = 48
COLS = 8 * HEAD
HALF = 3 * D // 2
PIECE = OWN + 3 * HEAD
BF = jnp.bfloat16
F32 = jnp.float32
SPACE = ("z", "y")
TENSOR = ("x", "core")
OFFS = (0, 3, 1, 2)
FIRST = 2 * 10**10
BACK = 3 * 10**10
TOKEN = 3 * 10**10


def dot(a, b, da, db):
    return lax.dot_general(a, b, (((da,), (db,)), ((), ())), preferred_element_type=F32)


def lanes(j):
    return pl.ds(pl.multiple_of(j * 128, 128), 128)


def call(body, name, outs, args, smem=(), scratch=(), flops=0, vmem=56, loose=()):
    specs = [
        pl.BlockSpec(
            memory_space=pltpu.SMEM if i in smem else pl.ANY if i in loose else pltpu.VMEM
        )
        for i in range(len(args))
    ]
    return pl.pallas_call(
        body,
        name=name,
        out_shape=tuple(jax.ShapeDtypeStruct(s, t) for s, t in outs),
        in_specs=specs,
        out_specs=tuple(pl.BlockSpec(memory_space=pltpu.VMEM) for _ in outs),
        scratch_shapes=list(scratch),
        compiler_params=pltpu.CompilerParams(vmem_limit_bytes=vmem * 2**20),
        cost_estimate=pl.CostEstimate(flops=flops, bytes_accessed=4 * 2**20, transcendentals=0),
    )(*args)


def prep_body(kinds, tokens, targets, second, head, out, packed):
    real = V * PP // 8
    row = lax.broadcasted_iota(jnp.int32, (HEAD, 128 - OWN), 0)
    kind = jnp.zeros(row.shape, F32)
    for v in range(V // 8):
        kind = jnp.where(row // PP == v, kinds[v].astype(F32), kind)
    blank = jnp.zeros((HEAD - real, 128), F32)
    packed[:D, :] = second[...]
    for i in range(8):
        out[i, :OWN, :] = tokens[OWN * i : OWN * (i + 1), :]
        rest = jnp.concatenate([targets[:, OWN * i : OWN * (i + 1)], kind[:real]], axis=1)
        rest = jnp.concatenate([rest, blank], axis=0)
        for piece in range(3):
            at = OWN + HEAD * piece
            part = rest.astype(BF)
            out[i, at : at + HEAD, :] = part
            rest = rest - part.astype(F32)
        rows = jnp.concatenate([head[:, 128 * i : 128 * (i + 1)].astype(F32), blank], axis=0)
        packed[D + HEAD * i : D + HEAD * (i + 1), :] = rows.astype(BF)


def gelu_parts(z):
    cdf = 0.5 * (1.0 + lax.erf(z * (1.0 / math.sqrt(2.0))))
    return z * cdf, cdf + z * jnp.exp(-0.5 * z * z) * (1.0 / math.sqrt(2.0 * math.pi))


def pairs(refs, rows=slice(0, D)):
    for a in range(2):
        for k in (0, 2):
            both = [refs[a][k, rows, :], refs[a][k + 1, rows, :]]
            yield jnp.concatenate(both, axis=1), 4 * a + k


def layer(idx, value, refs, pre):
    for both, at in pairs(refs):
        z = dot(value, both, 1, 0)
        pre[:, lanes(idx[at])] = z[:, :128]
        pre[:, lanes(idx[at + 1])] = z[:, 128:]
    return gelu_parts(pre[...])


def back_through(idx, grad, refs, rows=slice(0, D)):
    total = None
    for both, at in pairs(refs, rows):
        left = jnp.concatenate([grad[:, lanes(idx[at])], grad[:, lanes(idx[at + 1])]], axis=1)
        term = dot(left, both, 1, 1)
        total = term if total is None else total + term
    return total


def first_body(idx, given, near, far, tokhid, slope1, pre):
    for j in range(8):
        tokhid[:, 128 * j : 128 * (j + 1)] = given[j, :OWN, :]
    hidden, slope = layer(idx, tokhid[:, :D], (near, far), pre)
    tokhid[:, D:] = hidden.astype(BF)
    slope1[...] = slope


def second_body(
    idx, tokhid, given, near, far, land, weights, xh, slope2, me, sums, head, pre, goal
):
    for j in range(8):
        parts = [
            given[j, OWN + HEAD * p : OWN + HEAD * (p + 1), :].astype(F32) for p in range(3)
        ]
        goal[HEAD * j : HEAD * (j + 1), :] = parts[0] + (parts[1] + parts[2])
    for a, ref in enumerate((near, far)):
        for s in range(4):
            rows = pl.ds(pl.multiple_of(idx[4 * a + s] * HEAD, HEAD), HEAD)
            for i in range(8):
                piece = ref[s, D + HEAD * i : D + HEAD * (i + 1), :]
                head[rows, 128 * i : 128 * (i + 1)] = piece
    hidden, slope = layer(idx, tokhid[:, D:], (near, far), pre)
    hidden2 = hidden.astype(BF)
    xh[0] = tokhid[:, :HALF]
    xh[1, :, : 2 * D - HALF] = tokhid[:, HALF:]
    xh[1, :, 2 * D - HALF :] = hidden2
    slope2[...] = slope
    predicted = dot(hidden2, head[...], 1, 1)
    flipped = goal[...].T
    kind = flipped[OWN : OWN + 1, :]
    column = lax.broadcasted_iota(jnp.int32, (8, COLS), 1)
    picks = (column % PP == lax.broadcasted_iota(jnp.int32, (8, COLS), 0)).astype(BF)
    on_land = dot(land[...], picks, 0, 0)[:OWN, :]
    valid = jnp.where(kind == 0.0, 1.0, jnp.where(kind == 1.0, on_land, 1.0 - on_land))
    masked = weights[...] * valid
    error = predicted - flipped[:OWN, :]
    product = masked * error
    me[...] = product
    pair = [jnp.sum(product * error, axis=0, keepdims=True), jnp.sum(masked, axis=0, keepdims=True)]
    sums[...] = jnp.broadcast_to(jnp.concatenate(pair, axis=0)[None], sums.shape)


def over_cells(v):
    column = lax.broadcasted_iota(jnp.int32, v.shape, 1)
    n = v.shape[1]
    for step in (1, 2):
        ahead = pltpu.roll(v, n - step, 1)
        behind = pltpu.roll(v, step, 1)
        v = v + jnp.where((column // step) % 2 == 0, ahead, behind)
    return v


def backward_body(
    idx, scale, sums, me, slope1, slope2, head, near, far, joined, grad1, loss, g2
):
    total = over_cells(jnp.sum(sums[...], axis=0))
    column = lax.broadcasted_iota(jnp.int32, (1, COLS), 1)
    real = column % HEAD < V * PP // 8
    weight = jnp.where(real, total[1:2, :], 1.0)
    root = jnp.sqrt(total[0:1, :] / weight + 1e-06)
    loss[...] = jnp.sum(jnp.where(real, root, 0.0), axis=1, keepdims=True) / (V * PP)
    coef = jnp.where(real, scale[0] / (V * root * weight), 0.0)
    grad_pred = (coef * me[...]).astype(BF)
    g2[...] = (dot(grad_pred, head[...], 1, 0) * slope2[...]).astype(BF)
    back = back_through(idx, g2, (near, far))
    grad1[...] = (back * slope1[...]).astype(BF)
    for j in range(8):
        joined[j, :, :128] = g2[:, 128 * j : 128 * (j + 1)]
        joined[j, :, 128:256] = grad1[:, 128 * j : 128 * (j + 1)]
        tail = grad_pred[:, HEAD * j : HEAD * (j + 1)].astype(F32)
        tail = jnp.concatenate([tail, jnp.zeros((OWN, 128 - HEAD), F32)], axis=1)
        joined[j, :, 256:] = tail.astype(BF)


def token_body(idx, grad1, near, far, keep, send):
    grad = None
    for both, at in pairs((near, far)):
        left = jnp.concatenate([grad1[:, lanes(idx[at])], grad1[:, lanes(idx[at + 1])]], axis=1)
        term = dot(left, both, 1, 1)
        grad = term if grad is None else grad + term
    mine = idx[8] == 0
    for k in range(4):
        even, odd = grad[:, 256 * k : 256 * k + 128], grad[:, 256 * k + 128 : 256 * (k + 1)]
        keep[k] = jnp.where(mine, even, odd)
        send[k] = jnp.where(mine, odd, even)


def split_body(idx, keep, came, own, up, down, across):
    for ref, off in ((own, 0), (up, 1), (down, 3), (across, 2)):
        k = lax.rem(idx[9] + off, 4)
        ref[0] = keep[k]
        ref[1] = came[k]


def place_body(idx, own, left, right, across, out):
    for s, ref in enumerate((own, left, right, across)):
        for a in range(2):
            rows = pl.ds(pl.multiple_of(idx[4 * a + s] * OWN, OWN), OWN)
            out[rows, :] = ref[a]


def weight_body(idx, near, far, joined, out, order):
    for at in range(8):
        order[OWN * at : OWN * (at + 1), :] = joined[idx[at]]
    half = 4 * OWN
    sums = []
    places = (((1, 0, 512), (0, D, HALF)), ((0, 0, D),), ((1, 512, HALF),))
    for to, cuts in zip((0, 128, 256), (places[0][::-1], places[1], places[2])):
        found = []
        for h, lo, hi in cuts:
            term = dot(order[:half, to : to + 128], near[:, h, :, lo:hi].reshape(half, hi - lo), 0, 0)
            term += dot(order[half:, to : to + 128], far[:, h, :, lo:hi].reshape(half, hi - lo), 0, 0)
            found.append(term.T)
        sums.append(found[0] if len(found) == 1 else jnp.concatenate(found, axis=0))
    part = sums[2].reshape(64, 2, 8, 128)
    high = pltpu.roll(part[:, 1].reshape(512, 128), HEAD, 1).reshape(64, 8, 128)
    wide = [sums[0].reshape(64, 16, 128), sums[1].reshape(64, 16, 128), part[:, 0] + high]
    out[...] = jnp.concatenate(wide, axis=1).astype(BF)


def shift(v, by):
    return lax.ppermute(v, "x", [(i, (i + by) % 4) for i in range(4)])


def flip(v):
    return lax.ppermute(v, "core", [(0, 1), (1, 0)])


def per_device(
    tokens, first_weight, second_weight, head_weight, targets, land_mask, variable_kind, loss_scale
):
    x, core = lax.axis_index("x"), lax.axis_index("core")
    mine = lax.axis_index(TENSOR)
    places = [2 * ((x + off) % 4) + c for c in (core, 1 - core) for off in OFFS]
    idx = jnp.stack([*places, core, x]).astype(jnp.int32)

    land = lax.dynamic_slice(land_mask, (0, mine * OWN), (PP, OWN))
    land = jnp.pad(land.astype(BF), ((0, 8 - PP), (0, 128 - OWN)))
    space = lax.axis_index(SPACE)
    patch_row = (space * 8 * OWN + mine * OWN) // LONP
    nlat = 2 * (64 * 8 * OWN // LONP)
    col = jnp.arange(COLS, dtype=jnp.int32)
    lat_row = 2 * patch_row + (col % PP) // 2
    weights = jnp.cos(math.pi / 2.0 * (lat_row.astype(F32) + 0.5) / nlat)
    weights = jnp.where(col % HEAD < 44, weights, 0.0)[None, :]

    given, packed = call(
        prep_body, "prep", [((8, PIECE, 128), BF), ((D + COLS, 128), BF)],
        [variable_kind, tokens, targets, second_weight, head_weight], smem=(0,),
    )
    w1_m1, w1_p1 = shift(first_weight, 1), shift(first_weight, 3)
    w2_m1, w2_p1 = shift(packed, 1), shift(packed, 3)
    given, w1_m1 = lax.optimization_barrier((given, w1_m1))
    given = lax.all_to_all(given, TENSOR, 0, 0, tiled=True)
    w1_m1, w1_p1, w2_m1, w2_p1, idx, land, weights = lax.optimization_barrier(
        (w1_m1, w1_p1, w2_m1, w2_p1, idx, land, weights)
    )
    w1_last, w2_last = shift(w1_m1, 1), shift(w2_p1, 3)
    w1_last, w2_last, given = lax.optimization_barrier((w1_last, w2_last, given))
    near1 = jnp.stack([first_weight, w1_m1, w1_p1, w1_last])
    near2 = jnp.stack([packed, w2_m1, w2_p1, w2_last])
    far1, far2 = flip(near1), flip(near2)

    tokhid, slope1 = call(
        first_body, "first", [((OWN, 2 * D), BF), ((OWN, D), F32)], [idx, given, near1, far1],
        smem=(0,), scratch=[pltpu.VMEM((OWN, D), F32)], flops=FIRST,
    )
    xh, slope2, me, sums, head = call(
        second_body, "second",
        [((2, OWN, HALF), BF), ((OWN, D), F32), ((OWN, COLS), F32), ((8, 2, COLS), F32),
         ((COLS, D), BF)],
        [idx, tokhid, given, near2, far2, land, weights], smem=(0,),
        scratch=[pltpu.VMEM((OWN, D), F32), pltpu.VMEM((COLS, 128), F32)], flops=5 * 10**8,
    )

    sums = lax.all_to_all(sums, TENSOR, 0, 0, tiled=True)
    sums, xh = lax.optimization_barrier((sums, xh))
    spread = jnp.broadcast_to(jnp.sum(sums, axis=0), (64, 2, COLS))
    sums = lax.all_to_all(spread, SPACE, 0, 0, tiled=True)

    xh_m1, xh_p1 = shift(xh, 1), shift(xh, 3)
    xh_last = jnp.stack([shift(xh_m1[0], 1), shift(xh_p1[1], 3)])
    xhn = jnp.stack([xh, xh_m1, xh_p1, xh_last])
    xhf = flip(xhn)

    joined, grad1, loss = call(
        backward_body, "backward",
        [((8, OWN, 384), BF), ((OWN, D), BF), ((1, 1), F32)],
        [idx, loss_scale.reshape(1), sums, me, slope1, slope2, head, near2, far2],
        smem=(0, 1), scratch=[pltpu.VMEM((OWN, D), BF)], flops=BACK,
    )
    joined = lax.all_to_all(joined, TENSOR, 0, 0, tiled=True)
    (out,) = call(
        weight_body, "weight", [((64, 40, 128), BF)], [idx, xhn, xhf, joined], smem=(0,),
        scratch=[pltpu.VMEM((8 * OWN, 384), BF)], flops=8 * 10**8,
    )
    keep, send = call(
        token_body, "token", [((4, OWN, 128), F32)] * 2, [idx, grad1, near1, far1], smem=(0,),
        flops=TOKEN,
    )
    came, keep, out = lax.optimization_barrier((flip(send), keep, out))
    out = lax.all_to_all(out, SPACE, 0, 0, tiled=True)
    own, up, down, across = call(
        split_body, "split", [((2, OWN, 128), F32)] * 4, [idx, keep, came], smem=(0,)
    )
    (token_grad,) = call(
        place_body, "place", [((8 * OWN, 128), F32)],
        [idx, own, shift(up, 1), shift(down, 3), shift(across, 2)], smem=(0,),
    )
    out = jnp.sum(out.astype(F32), axis=0)
    halves = jnp.concatenate([out[32:, :44], out[32:, HEAD : HEAD + 44]], axis=0)
    return loss.reshape(()), token_grad, out[16:32], out[:16], halves.T


def solution(mesh):
    inner = Mesh(mesh.devices.reshape(8, 8, 4, 2), ("z", "y", "x", "core"))
    return jax.shard_map(
        per_device,
        mesh=inner,
        in_specs=(
            P(SPACE, TENSOR),
            P(None, TENSOR),
            P(None, TENSOR),
            P(TENSOR, None),
            P(TENSOR, SPACE),
            P(None, SPACE),
            P(TENSOR),
            P(),
        ),
        out_specs=(
            P(),
            P(SPACE, TENSOR),
            P(SPACE, TENSOR),
            P(SPACE, TENSOR),
            P(TENSOR, SPACE),
        ),
        check_vma=False,
    )
```

```python
import math

import jax
import jax.numpy as jnp
from jax import lax
from jax.experimental import pallas as pl
from jax.experimental.pallas import tpu as pltpu
from jax.sharding import Mesh
from jax.sharding import PartitionSpec as P

V = 88
PP = 4
LONP = 224
D = 1024
OWN = 112
HEAD = 48
COLS = 8 * HEAD
HALF = 3 * D // 2
PIECE = OWN + 3 * HEAD
BF = jnp.bfloat16
F32 = jnp.float32
SPACE = ("z", "y")
TENSOR = ("x", "core")
OFFS = (0, 3, 1, 2)
FIRST = 2 * 10**10
BACK = 3 * 10**10
TOKEN = 3 * 10**10


def dot(a, b, da, db):
    return lax.dot_general(a, b, (((da,), (db,)), ((), ())), preferred_element_type=F32)


def lanes(j):
    return pl.ds(pl.multiple_of(j * 128, 128), 128)


def call(body, name, outs, args, smem=(), scratch=(), flops=0, vmem=56, loose=()):
    specs = [
        pl.BlockSpec(
            memory_space=pltpu.SMEM if i in smem else pl.ANY if i in loose else pltpu.VMEM
        )
        for i in range(len(args))
    ]
    return pl.pallas_call(
        body,
        name=name,
        out_shape=tuple(jax.ShapeDtypeStruct(s, t) for s, t in outs),
        in_specs=specs,
        out_specs=tuple(pl.BlockSpec(memory_space=pltpu.VMEM) for _ in outs),
        scratch_shapes=list(scratch),
        compiler_params=pltpu.CompilerParams(vmem_limit_bytes=vmem * 2**20),
        cost_estimate=pl.CostEstimate(flops=flops, bytes_accessed=4 * 2**20, transcendentals=0),
    )(*args)


def prep_body(kinds, tokens, targets, second, head, out, packed):
    real = V * PP // 8
    row = lax.broadcasted_iota(jnp.int32, (HEAD, 128 - OWN), 0)
    kind = jnp.zeros(row.shape, F32)
    for v in range(V // 8):
        kind = jnp.where(row // PP == v, kinds[v].astype(F32), kind)
    blank = jnp.zeros((HEAD - real, 128), F32)
    packed[:D, :] = second[...]
    for i in range(8):
        out[i, :OWN, :] = tokens[OWN * i : OWN * (i + 1), :]
        rest = jnp.concatenate([targets[:, OWN * i : OWN * (i + 1)], kind[:real]], axis=1)
        rest = jnp.concatenate([rest, blank], axis=0)
        for piece in range(3):
            at = OWN + HEAD * piece
            part = rest.astype(BF)
            out[i, at : at + HEAD, :] = part
            rest = rest - part.astype(F32)
        rows = jnp.concatenate([head[:, 128 * i : 128 * (i + 1)].astype(F32), blank], axis=0)
        packed[D + HEAD * i : D + HEAD * (i + 1), :] = rows.astype(BF)


def gelu_parts(z):
    cdf = 0.5 * (1.0 + lax.erf(z * (1.0 / math.sqrt(2.0))))
    return z * cdf, cdf + z * jnp.exp(-0.5 * z * z) * (1.0 / math.sqrt(2.0 * math.pi))


def room(shape):
    return [pltpu.VMEM(shape, BF), pltpu.VMEM(shape, BF), pltpu.SemaphoreType.DMA((2,))]


def fetch(sources, targets, sems):
    copies = [
        pltpu.make_async_copy(src, dst, sems.at[i])
        for i, (src, dst) in enumerate(zip(sources, targets))
    ]
    for copy in copies:
        copy.start()
    return copies


def pairs(refs, rows=slice(0, D), copies=None):
    for a in range(2):
        if copies:
            copies[a].wait()
        for k in (0, 2):
            both = [refs[a][k, rows, :], refs[a][k + 1, rows, :]]
            yield jnp.concatenate(both, axis=1), 4 * a + k


def layer(idx, value, refs, pre, copies):
    for both, at in pairs(refs, copies=copies):
        z = dot(value, both, 1, 0)
        pre[:, lanes(idx[at])] = z[:, :128]
        pre[:, lanes(idx[at + 1])] = z[:, 128:]
    return gelu_parts(pre[...])


def back_through(idx, grad, refs, copies):
    total = None
    for both, at in pairs(refs, copies=copies):
        left = jnp.concatenate([grad[:, lanes(idx[at])], grad[:, lanes(idx[at + 1])]], axis=1)
        term = dot(left, both, 1, 1)
        total = term if total is None else total + term
    return total


def first_body(idx, given, near_at, far_at, tokhid, slope1, pre, near, far, sems):
    copies = fetch((near_at, far_at), (near, far), sems)
    for j in range(8):
        tokhid[:, 128 * j : 128 * (j + 1)] = given[j, :OWN, :]
    hidden, slope = layer(idx, tokhid[:, :D], (near, far), pre, copies)
    tokhid[:, D:] = hidden.astype(BF)
    slope1[...] = slope


def second_body(
    idx, tokhid, given, near_at, far_at, land, weights,
    xh, slope2, me, sums, head, pre, goal, near, far, sems,
):
    copies = fetch((near_at, far_at), (near, far), sems)
    for j in range(8):
        parts = [
            given[j, OWN + HEAD * p : OWN + HEAD * (p + 1), :].astype(F32) for p in range(3)
        ]
        goal[HEAD * j : HEAD * (j + 1), :] = parts[0] + (parts[1] + parts[2])
    hidden, slope = layer(idx, tokhid[:, D:], (near, far), pre, copies)
    for a, ref in enumerate((near, far)):
        for s in range(4):
            rows = pl.ds(pl.multiple_of(idx[4 * a + s] * HEAD, HEAD), HEAD)
            for i in range(8):
                piece = ref[s, D + HEAD * i : D + HEAD * (i + 1), :]
                head[rows, 128 * i : 128 * (i + 1)] = piece
    hidden2 = hidden.astype(BF)
    xh[0] = tokhid[:, :HALF]
    xh[1, :, : 2 * D - HALF] = tokhid[:, HALF:]
    xh[1, :, 2 * D - HALF :] = hidden2
    slope2[...] = slope
    predicted = dot(hidden2, head[...], 1, 1)
    flipped = goal[...].T
    kind = flipped[OWN : OWN + 1, :]
    column = lax.broadcasted_iota(jnp.int32, (8, COLS), 1)
    picks = (column % PP == lax.broadcasted_iota(jnp.int32, (8, COLS), 0)).astype(BF)
    on_land = dot(land[...], picks, 0, 0)[:OWN, :]
    valid = jnp.where(kind == 0.0, 1.0, jnp.where(kind == 1.0, on_land, 1.0 - on_land))
    masked = weights[...] * valid
    error = predicted - flipped[:OWN, :]
    product = masked * error
    me[...] = product
    pair = [jnp.sum(product * error, axis=0, keepdims=True), jnp.sum(masked, axis=0, keepdims=True)]
    sums[...] = jnp.broadcast_to(jnp.concatenate(pair, axis=0)[None], sums.shape)


def over_cells(v):
    column = lax.broadcasted_iota(jnp.int32, v.shape, 1)
    n = v.shape[1]
    for step in (1, 2):
        ahead = pltpu.roll(v, n - step, 1)
        behind = pltpu.roll(v, step, 1)
        v = v + jnp.where((column // step) % 2 == 0, ahead, behind)
    return v


def backward_body(
    idx, scale, sums, me, slope1, slope2, head, near_at, far_at,
    joined, grad1, loss, g2, near, far, sems,
):
    copies = fetch((near_at, far_at), (near, far), sems)
    total = over_cells(jnp.sum(sums[...], axis=0))
    column = lax.broadcasted_iota(jnp.int32, (1, COLS), 1)
    real = column % HEAD < V * PP // 8
    weight = jnp.where(real, total[1:2, :], 1.0)
    root = jnp.sqrt(total[0:1, :] / weight + 1e-06)
    loss[...] = jnp.sum(jnp.where(real, root, 0.0), axis=1, keepdims=True) / (V * PP)
    coef = jnp.where(real, scale[0] / (V * root * weight), 0.0)
    grad_pred = (coef * me[...]).astype(BF)
    g2[...] = (dot(grad_pred, head[...], 1, 0) * slope2[...]).astype(BF)
    back = back_through(idx, g2, (near, far), copies)
    grad1[...] = (back * slope1[...]).astype(BF)
    for j in range(8):
        joined[j, :, :128] = g2[:, 128 * j : 128 * (j + 1)]
        joined[j, :, 128:256] = grad1[:, 128 * j : 128 * (j + 1)]
        tail = grad_pred[:, HEAD * j : HEAD * (j + 1)].astype(F32)
        tail = jnp.concatenate([tail, jnp.zeros((OWN, 128 - HEAD), F32)], axis=1)
        joined[j, :, 256:] = tail.astype(BF)


def token_body(idx, grad1, near, far, keep, send):
    grad = None
    for both, at in pairs((near, far)):
        left = jnp.concatenate([grad1[:, lanes(idx[at])], grad1[:, lanes(idx[at + 1])]], axis=1)
        term = dot(left, both, 1, 1)
        grad = term if grad is None else grad + term
    mine = idx[8] == 0
    for k in range(4):
        even, odd = grad[:, 256 * k : 256 * k + 128], grad[:, 256 * k + 128 : 256 * (k + 1)]
        keep[k] = jnp.where(mine, even, odd)
        send[k] = jnp.where(mine, odd, even)


def split_body(idx, keep, came, own, up, down, across):
    for ref, off in ((own, 0), (up, 1), (down, 3), (across, 2)):
        k = lax.rem(idx[9] + off, 4)
        ref[0] = keep[k]
        ref[1] = came[k]


def place_body(idx, own, left, right, across, out):
    for s, ref in enumerate((own, left, right, across)):
        for a in range(2):
            rows = pl.ds(pl.multiple_of(idx[4 * a + s] * OWN, OWN), OWN)
            out[rows, :] = ref[a]


def weight_body(idx, near_at, far_at, joined, out, order, near, far, sems):
    copies = fetch((near_at, far_at), (near, far), sems)
    for at in range(8):
        order[OWN * at : OWN * (at + 1), :] = joined[idx[at]]
    half = 4 * OWN
    cuts = ((0, 0, D, HALF), (0, 1, 0, 512), (128, 0, 0, D), (256, 1, 512, HALF))
    found = [0.0] * 4
    for copy, ref, left in ((copies[0], near, order[:half]), (copies[1], far, order[half:])):
        copy.wait()
        for i, (to, h, lo, hi) in enumerate(cuts):
            right = ref[:, h, :, lo:hi].reshape(half, hi - lo)
            found[i] = found[i] + dot(left[:, to : to + 128], right, 0, 0)
    sums = [jnp.concatenate([found[0].T, found[1].T], axis=0), found[2].T, found[3].T]
    part = sums[2].reshape(64, 2, 8, 128)
    high = pltpu.roll(part[:, 1].reshape(512, 128), HEAD, 1).reshape(64, 8, 128)
    wide = [sums[0].reshape(64, 16, 128), sums[1].reshape(64, 16, 128), part[:, 0] + high]
    out[...] = jnp.concatenate(wide, axis=1).astype(BF)


def shift(v, by):
    return lax.ppermute(v, "x", [(i, (i + by) % 4) for i in range(4)])


def flip(v):
    return lax.ppermute(v, "core", [(0, 1), (1, 0)])


def per_device(
    tokens, first_weight, second_weight, head_weight, targets, land_mask, variable_kind, loss_scale
):
    x, core = lax.axis_index("x"), lax.axis_index("core")
    mine = lax.axis_index(TENSOR)
    places = [2 * ((x + off) % 4) + c for c in (core, 1 - core) for off in OFFS]
    idx = jnp.stack([*places, core, x]).astype(jnp.int32)

    land = lax.dynamic_slice(land_mask, (0, mine * OWN), (PP, OWN))
    land = jnp.pad(land.astype(BF), ((0, 8 - PP), (0, 128 - OWN)))
    space = lax.axis_index(SPACE)
    patch_row = (space * 8 * OWN + mine * OWN) // LONP
    nlat = 2 * (64 * 8 * OWN // LONP)
    col = jnp.arange(COLS, dtype=jnp.int32)
    lat_row = 2 * patch_row + (col % PP) // 2
    weights = jnp.cos(math.pi / 2.0 * (lat_row.astype(F32) + 0.5) / nlat)
    weights = jnp.where(col % HEAD < 44, weights, 0.0)[None, :]

    given, packed = call(
        prep_body, "prep", [((8, PIECE, 128), BF), ((D + COLS, 128), BF)],
        [variable_kind, tokens, targets, second_weight, head_weight], smem=(0,),
    )
    w1_m1, w1_p1 = shift(first_weight, 1), shift(first_weight, 3)
    w2_m1, w2_p1 = shift(packed, 1), shift(packed, 3)
    given, w1_m1 = lax.optimization_barrier((given, w1_m1))
    given = lax.all_to_all(given, TENSOR, 0, 0, tiled=True)
    w1_m1, w1_p1, w2_m1, w2_p1, idx, land, weights = lax.optimization_barrier(
        (w1_m1, w1_p1, w2_m1, w2_p1, idx, land, weights)
    )
    w1_last, w2_last = shift(w1_m1, 1), shift(w2_p1, 3)
    w1_last, w2_last, given = lax.optimization_barrier((w1_last, w2_last, given))
    near1 = jnp.stack([first_weight, w1_m1, w1_p1, w1_last])
    near2 = jnp.stack([packed, w2_m1, w2_p1, w2_last])
    far1, far2 = flip(near1), flip(near2)

    tokhid, slope1 = call(
        first_body, "first", [((OWN, 2 * D), BF), ((OWN, D), F32)], [idx, given, near1, far1],
        smem=(0,), loose=(2, 3),
        scratch=[pltpu.VMEM((OWN, D), F32), *room((4, D, 128))], flops=FIRST,
    )
    xh, slope2, me, sums, head = call(
        second_body, "second",
        [((2, OWN, HALF), BF), ((OWN, D), F32), ((OWN, COLS), F32), ((8, 2, COLS), F32),
         ((COLS, D), BF)],
        [idx, tokhid, given, near2, far2, land, weights], smem=(0,), loose=(3, 4), flops=5 * 10**8,
        scratch=[pltpu.VMEM((OWN, D), F32), pltpu.VMEM((COLS, 128), F32), *room((4, D + COLS, 128))],
    )

    sums = lax.all_to_all(sums, TENSOR, 0, 0, tiled=True)
    sums, xh = lax.optimization_barrier((sums, xh))
    spread = jnp.broadcast_to(jnp.sum(sums, axis=0), (64, 2, COLS))
    sums = lax.all_to_all(spread, SPACE, 0, 0, tiled=True)

    xh_m1, xh_p1 = shift(xh, 1), shift(xh, 3)
    xh_last = jnp.stack([shift(xh_m1[0], 1), shift(xh_p1[1], 3)])
    xhn = jnp.stack([xh, xh_m1, xh_p1, xh_last])
    xhf = flip(xhn)

    joined, grad1, loss = call(
        backward_body, "backward",
        [((8, OWN, 384), BF), ((OWN, D), BF), ((1, 1), F32)],
        [idx, loss_scale.reshape(1), sums, me, slope1, slope2, head, near2, far2],
        smem=(0, 1), loose=(7, 8), flops=BACK,
        scratch=[pltpu.VMEM((OWN, D), BF), *room((4, D + COLS, 128))],
    )
    joined = lax.all_to_all(joined, TENSOR, 0, 0, tiled=True)
    (out,) = call(
        weight_body, "weight", [((64, 40, 128), BF)], [idx, xhn, xhf, joined], smem=(0,),
        loose=(1, 2), flops=8 * 10**8,
        scratch=[pltpu.VMEM((8 * OWN, 384), BF), *room((4, 2, OWN, HALF))],
    )
    keep, send = call(
        token_body, "token", [((4, OWN, 128), F32)] * 2, [idx, grad1, near1, far1], smem=(0,),
        flops=TOKEN,
    )
    came, keep, out = lax.optimization_barrier((flip(send), keep, out))
    out = lax.all_to_all(out, SPACE, 0, 0, tiled=True)
    own, up, down, across = call(
        split_body, "split", [((2, OWN, 128), F32)] * 4, [idx, keep, came], smem=(0,)
    )
    (token_grad,) = call(
        place_body, "place", [((8 * OWN, 128), F32)],
        [idx, own, shift(up, 1), shift(down, 3), shift(across, 2)], smem=(0,),
    )
    out = jnp.sum(out.astype(F32), axis=0)
    halves = jnp.concatenate([out[32:, :44], out[32:, HEAD : HEAD + 44]], axis=0)
    return loss.reshape(()), token_grad, out[16:32], out[:16], halves.T


def solution(mesh):
    inner = Mesh(mesh.devices.reshape(8, 8, 4, 2), ("z", "y", "x", "core"))
    return jax.shard_map(
        per_device,
        mesh=inner,
        in_specs=(
            P(SPACE, TENSOR),
            P(None, TENSOR),
            P(None, TENSOR),
            P(TENSOR, None),
            P(TENSOR, SPACE),
            P(None, SPACE),
            P(TENSOR),
            P(),
        ),
        out_specs=(
            P(),
            P(SPACE, TENSOR),
            P(SPACE, TENSOR),
            P(SPACE, TENSOR),
            P(TENSOR, SPACE),
        ),
        check_vma=False,
    )
```

```python
import math

import jax
import jax.numpy as jnp
from jax import lax
from jax.experimental import pallas as pl
from jax.experimental.pallas import tpu as pltpu
from jax.sharding import Mesh
from jax.sharding import PartitionSpec as P

V = 88
PP = 4
LONP = 224
D = 1024
OWN = 112
HEAD = 48
COLS = 8 * HEAD
HALF = 3 * D // 2
PIECE = OWN + 3 * HEAD
BF = jnp.bfloat16
F32 = jnp.float32
SPACE = ("z", "y")
TENSOR = ("x", "core")
OFFS = (0, 3, 1, 2)
FIRST = 2 * 10**10
BACK = 3 * 10**10
TOKEN = 3 * 10**10


def dot(a, b, da, db):
    return lax.dot_general(a, b, (((da,), (db,)), ((), ())), preferred_element_type=F32)


def lanes(j):
    return pl.ds(pl.multiple_of(j * 128, 128), 128)


def call(body, name, outs, args, smem=(), scratch=(), flops=0, vmem=28, loose=()):
    specs = [
        pl.BlockSpec(
            memory_space=pltpu.SMEM if i in smem else pl.ANY if i in loose else pltpu.VMEM
        )
        for i in range(len(args))
    ]
    return pl.pallas_call(
        body,
        name=name,
        out_shape=tuple(jax.ShapeDtypeStruct(s, t) for s, t in outs),
        in_specs=specs,
        out_specs=tuple(pl.BlockSpec(memory_space=pltpu.VMEM) for _ in outs),
        scratch_shapes=list(scratch),
        compiler_params=pltpu.CompilerParams(vmem_limit_bytes=vmem * 2**20),
        cost_estimate=pl.CostEstimate(flops=flops, bytes_accessed=4 * 2**20, transcendentals=0),
    )(*args)


def prep_body(kinds, tokens, targets, second, head, out, packed):
    real = V * PP // 8
    row = lax.broadcasted_iota(jnp.int32, (HEAD, 128 - OWN), 0)
    kind = jnp.zeros(row.shape, F32)
    for v in range(V // 8):
        kind = jnp.where(row // PP == v, kinds[v].astype(F32), kind)
    blank = jnp.zeros((HEAD - real, 128), F32)
    packed[:D, :] = second[...]
    for i in range(8):
        out[i, :OWN, :] = tokens[OWN * i : OWN * (i + 1), :]
        rest = jnp.concatenate([targets[:, OWN * i : OWN * (i + 1)], kind[:real]], axis=1)
        rest = jnp.concatenate([rest, blank], axis=0)
        for piece in range(3):
            at = OWN + HEAD * piece
            part = rest.astype(BF)
            out[i, at : at + HEAD, :] = part
            rest = rest - part.astype(F32)
        rows = jnp.concatenate([head[:, 128 * i : 128 * (i + 1)].astype(F32), blank], axis=0)
        packed[D + HEAD * i : D + HEAD * (i + 1), :] = rows.astype(BF)


def gelu_parts(z):
    cdf = 0.5 * (1.0 + lax.erf(z * (1.0 / math.sqrt(2.0))))
    return z * cdf, cdf + z * jnp.exp(-0.5 * z * z) * (1.0 / math.sqrt(2.0 * math.pi))


def pairs(refs, rows=slice(0, D)):
    for a in range(2):
        for k in (0, 2):
            both = [refs[a][k, rows, :], refs[a][k + 1, rows, :]]
            yield jnp.concatenate(both, axis=1), 4 * a + k


def layer(idx, value, refs, pre):
    for both, at in pairs(refs):
        z = dot(value, both, 1, 0)
        pre[:, lanes(idx[at])] = z[:, :128]
        pre[:, lanes(idx[at + 1])] = z[:, 128:]
    return gelu_parts(pre[...])


def back_through(idx, grad, refs, rows=slice(0, D)):
    total = None
    for both, at in pairs(refs, rows):
        left = jnp.concatenate([grad[:, lanes(idx[at])], grad[:, lanes(idx[at + 1])]], axis=1)
        term = dot(left, both, 1, 1)
        total = term if total is None else total + term
    return total


def first_body(idx, given, near, far, tokhid, slope1, pre):
    for j in range(8):
        tokhid[:, 128 * j : 128 * (j + 1)] = given[j, :OWN, :]
    hidden, slope = layer(idx, tokhid[:, :D], (near, far), pre)
    tokhid[:, D:] = hidden.astype(BF)
    slope1[...] = slope


def second_body(
    idx, tokhid, given, near, far, land, weights, xh, slope2, me, sums, head, pre, goal
):
    for j in range(8):
        parts = [
            given[j, OWN + HEAD * p : OWN + HEAD * (p + 1), :].astype(F32) for p in range(3)
        ]
        goal[HEAD * j : HEAD * (j + 1), :] = parts[0] + (parts[1] + parts[2])
    for a, ref in enumerate((near, far)):
        for s in range(4):
            rows = pl.ds(pl.multiple_of(idx[4 * a + s] * HEAD, HEAD), HEAD)
            for i in range(8):
                piece = ref[s, D + HEAD * i : D + HEAD * (i + 1), :]
                head[rows, 128 * i : 128 * (i + 1)] = piece
    hidden, slope = layer(idx, tokhid[:, D:], (near, far), pre)
    hidden2 = hidden.astype(BF)
    xh[0] = tokhid[:, :HALF]
    xh[1, :, : 2 * D - HALF] = tokhid[:, HALF:]
    xh[1, :, 2 * D - HALF :] = hidden2
    slope2[...] = slope
    predicted = dot(hidden2, head[...], 1, 1)
    flipped = goal[...].T
    kind = flipped[OWN : OWN + 1, :]
    column = lax.broadcasted_iota(jnp.int32, (8, COLS), 1)
    picks = (column % PP == lax.broadcasted_iota(jnp.int32, (8, COLS), 0)).astype(BF)
    on_land = dot(land[...], picks, 0, 0)[:OWN, :]
    valid = jnp.where(kind == 0.0, 1.0, jnp.where(kind == 1.0, on_land, 1.0 - on_land))
    masked = weights[...] * valid
    error = predicted - flipped[:OWN, :]
    product = masked * error
    me[...] = product
    pair = [jnp.sum(product * error, axis=0, keepdims=True), jnp.sum(masked, axis=0, keepdims=True)]
    sums[...] = jnp.broadcast_to(jnp.concatenate(pair, axis=0)[None], sums.shape)


def over_cells(v):
    column = lax.broadcasted_iota(jnp.int32, v.shape, 1)
    n = v.shape[1]
    for step in (1, 2):
        ahead = pltpu.roll(v, n - step, 1)
        behind = pltpu.roll(v, step, 1)
        v = v + jnp.where((column // step) % 2 == 0, ahead, behind)
    return v


def backward_body(
    idx, scale, sums, me, slope1, slope2, head, near, far, joined, grad1, loss, g2
):
    total = over_cells(jnp.sum(sums[...], axis=0))
    column = lax.broadcasted_iota(jnp.int32, (1, COLS), 1)
    real = column % HEAD < V * PP // 8
    weight = jnp.where(real, total[1:2, :], 1.0)
    root = jnp.sqrt(total[0:1, :] / weight + 1e-06)
    loss[...] = jnp.sum(jnp.where(real, root, 0.0), axis=1, keepdims=True) / (V * PP)
    coef = jnp.where(real, scale[0] / (V * root * weight), 0.0)
    grad_pred = (coef * me[...]).astype(BF)
    g2[...] = (dot(grad_pred, head[...], 1, 0) * slope2[...]).astype(BF)
    back = back_through(idx, g2, (near, far))
    grad1[...] = (back * slope1[...]).astype(BF)
    for j in range(8):
        joined[j, :, :128] = g2[:, 128 * j : 128 * (j + 1)]
        joined[j, :, 128:256] = grad1[:, 128 * j : 128 * (j + 1)]
        tail = grad_pred[:, HEAD * j : HEAD * (j + 1)].astype(F32)
        tail = jnp.concatenate([tail, jnp.zeros((OWN, 128 - HEAD), F32)], axis=1)
        joined[j, :, 256:] = tail.astype(BF)


def token_body(idx, grad1, near, far, keep, send):
    grad = None
    for both, at in pairs((near, far)):
        left = jnp.concatenate([grad1[:, lanes(idx[at])], grad1[:, lanes(idx[at + 1])]], axis=1)
        term = dot(left, both, 1, 1)
        grad = term if grad is None else grad + term
    mine = idx[8] == 0
    for k in range(4):
        even, odd = grad[:, 256 * k : 256 * k + 128], grad[:, 256 * k + 128 : 256 * (k + 1)]
        keep[k] = jnp.where(mine, even, odd)
        send[k] = jnp.where(mine, odd, even)


def split_body(idx, keep, came, own, up, down, across):
    for ref, off in ((own, 0), (up, 1), (down, 3), (across, 2)):
        k = lax.rem(idx[9] + off, 4)
        ref[0] = keep[k]
        ref[1] = came[k]


def place_body(idx, own, left, right, across, out):
    for s, ref in enumerate((own, left, right, across)):
        for a in range(2):
            rows = pl.ds(pl.multiple_of(idx[4 * a + s] * OWN, OWN), OWN)
            out[rows, :] = ref[a]


def weight_body(idx, near, far, joined, out, order):
    for at in range(8):
        order[OWN * at : OWN * (at + 1), :] = joined[idx[at]]
    half = 4 * OWN
    sums = []
    places = (((1, 0, 512), (0, D, HALF)), ((0, 0, D),), ((1, 512, HALF),))
    for to, cuts in zip((0, 128, 256), (places[0][::-1], places[1], places[2])):
        found = []
        for h, lo, hi in cuts:
            term = dot(order[:half, to : to + 128], near[:, h, :, lo:hi].reshape(half, hi - lo), 0, 0)
            term += dot(order[half:, to : to + 128], far[:, h, :, lo:hi].reshape(half, hi - lo), 0, 0)
            found.append(term.T)
        sums.append(found[0] if len(found) == 1 else jnp.concatenate(found, axis=0))
    part = sums[2].reshape(64, 2, 8, 128)
    high = pltpu.roll(part[:, 1].reshape(512, 128), HEAD, 1).reshape(64, 8, 128)
    wide = [sums[0].reshape(64, 16, 128), sums[1].reshape(64, 16, 128), part[:, 0] + high]
    out[...] = jnp.concatenate(wide, axis=1).astype(BF)


def shift(v, by):
    return lax.ppermute(v, "x", [(i, (i + by) % 4) for i in range(4)])


def flip(v):
    return lax.ppermute(v, "core", [(0, 1), (1, 0)])


def per_device(
    tokens, first_weight, second_weight, head_weight, targets, land_mask, variable_kind, loss_scale
):
    x, core = lax.axis_index("x"), lax.axis_index("core")
    mine = lax.axis_index(TENSOR)
    places = [2 * ((x + off) % 4) + c for c in (core, 1 - core) for off in OFFS]
    idx = jnp.stack([*places, core, x]).astype(jnp.int32)

    land = lax.dynamic_slice(land_mask, (0, mine * OWN), (PP, OWN))
    land = jnp.pad(land.astype(BF), ((0, 8 - PP), (0, 128 - OWN)))
    space = lax.axis_index(SPACE)
    patch_row = (space * 8 * OWN + mine * OWN) // LONP
    nlat = 2 * (64 * 8 * OWN // LONP)
    col = jnp.arange(COLS, dtype=jnp.int32)
    lat_row = 2 * patch_row + (col % PP) // 2
    weights = jnp.cos(math.pi / 2.0 * (lat_row.astype(F32) + 0.5) / nlat)
    weights = jnp.where(col % HEAD < 44, weights, 0.0)[None, :]

    given, packed = call(
        prep_body, "prep", [((8, PIECE, 128), BF), ((D + COLS, 128), BF)],
        [variable_kind, tokens, targets, second_weight, head_weight], smem=(0,),
    )
    w1_m1, w1_p1 = shift(first_weight, 1), shift(first_weight, 3)
    w2_m1, w2_p1 = shift(packed, 1), shift(packed, 3)
    given, w1_m1 = lax.optimization_barrier((given, w1_m1))
    given = lax.all_to_all(given, TENSOR, 0, 0, tiled=True)
    w1_m1, w1_p1, w2_m1, w2_p1, idx, land, weights = lax.optimization_barrier(
        (w1_m1, w1_p1, w2_m1, w2_p1, idx, land, weights)
    )
    w1_last, w2_last = shift(w1_m1, 1), shift(w2_p1, 3)
    w1_last, w2_last, given = lax.optimization_barrier((w1_last, w2_last, given))
    near1 = jnp.stack([first_weight, w1_m1, w1_p1, w1_last])
    near2 = jnp.stack([packed, w2_m1, w2_p1, w2_last])
    far1, far2 = flip(near1), flip(near2)

    tokhid, slope1 = call(
        first_body, "first", [((OWN, 2 * D), BF), ((OWN, D), F32)], [idx, given, near1, far1],
        smem=(0,), scratch=[pltpu.VMEM((OWN, D), F32)], flops=FIRST,
    )
    xh, slope2, me, sums, head = call(
        second_body, "second",
        [((2, OWN, HALF), BF), ((OWN, D), F32), ((OWN, COLS), F32), ((8, 2, COLS), F32),
         ((COLS, D), BF)],
        [idx, tokhid, given, near2, far2, land, weights], smem=(0,),
        scratch=[pltpu.VMEM((OWN, D), F32), pltpu.VMEM((COLS, 128), F32)], flops=5 * 10**8,
    )

    sums = lax.all_to_all(sums, TENSOR, 0, 0, tiled=True)
    sums, xh = lax.optimization_barrier((sums, xh))
    spread = jnp.broadcast_to(jnp.sum(sums, axis=0), (64, 2, COLS))
    sums = lax.all_to_all(spread, SPACE, 0, 0, tiled=True)

    xh_m1, xh_p1 = shift(xh, 1), shift(xh, 3)
    xh_last = jnp.stack([shift(xh_m1[0], 1), shift(xh_p1[1], 3)])
    xhn = jnp.stack([xh, xh_m1, xh_p1, xh_last])
    xhf = flip(xhn)

    joined, grad1, loss = call(
        backward_body, "backward",
        [((8, OWN, 384), BF), ((OWN, D), BF), ((1, 1), F32)],
        [idx, loss_scale.reshape(1), sums, me, slope1, slope2, head, near2, far2],
        smem=(0, 1), scratch=[pltpu.VMEM((OWN, D), BF)], flops=BACK,
    )
    joined = lax.all_to_all(joined, TENSOR, 0, 0, tiled=True)
    (out,) = call(
        weight_body, "weight", [((64, 40, 128), BF)], [idx, xhn, xhf, joined], smem=(0,),
        scratch=[pltpu.VMEM((8 * OWN, 384), BF)], flops=8 * 10**8,
    )
    keep, send = call(
        token_body, "token", [((4, OWN, 128), F32)] * 2, [idx, grad1, near1, far1], smem=(0,),
        flops=TOKEN,
    )
    came, keep, out = lax.optimization_barrier((flip(send), keep, out))
    out = lax.all_to_all(out, SPACE, 0, 0, tiled=True)
    own, up, down, across = call(
        split_body, "split", [((2, OWN, 128), F32)] * 4, [idx, keep, came], smem=(0,)
    )
    (token_grad,) = call(
        place_body, "place", [((8 * OWN, 128), F32)],
        [idx, own, shift(up, 1), shift(down, 3), shift(across, 2)], smem=(0,),
    )
    out = jnp.sum(out.astype(F32), axis=0)
    halves = jnp.concatenate([out[32:, :44], out[32:, HEAD : HEAD + 44]], axis=0)
    return loss.reshape(()), token_grad, out[16:32], out[:16], halves.T


def solution(mesh):
    inner = Mesh(mesh.devices.reshape(8, 8, 4, 2), ("z", "y", "x", "core"))
    return jax.shard_map(
        per_device,
        mesh=inner,
        in_specs=(
            P(SPACE, TENSOR),
            P(None, TENSOR),
            P(None, TENSOR),
            P(TENSOR, None),
            P(TENSOR, SPACE),
            P(None, SPACE),
            P(TENSOR),
            P(),
        ),
        out_specs=(
            P(),
            P(SPACE, TENSOR),
            P(SPACE, TENSOR),
            P(SPACE, TENSOR),
            P(TENSOR, SPACE),
        ),
        check_vma=False,
    )
```
